32 devices in a mesh: ens: 2 (over x), tile: 16 (over z, y, core).
Axes of the slice: x: 2, y: 2, z: 4, core: 2. Of those that a mesh axis runs over, the one named last changes fastest.
Arguments:
- fields: bfloat16 [2, 16, 64, 16, 128], P('ens', 'tile'), may hold values from -6 to 6
- cotangent: bfloat16 [2, 16, 64, 16, 128], P('ens', 'tile'), may hold values from -6 to 6
- kernel_first: bfloat16 [9, 64, 64], replicated, may hold values from -0.25 to 0.25
- kernel_second: bfloat16 [9, 128, 64], replicated, may hold values from -0.25 to 0.25
- kernel_third: bfloat16 [9, 128, 128], replicated, may hold values from -0.1875 to 0.1875
- closing_filter_weights: bfloat16 [9, 64, 192], replicated, may hold values from -0.15625 to 0.15625
- offset_first: float32 [64], replicated, may hold values from -3 to 3
- offset_second: float32 [128], replicated, may hold values from -3 to 3
- offset_third: float32 [128], replicated, may hold values from -3 to 3
- closing_shift_values: float32 [64], replicated, may hold values from -3 to 3
- codes: int32 [16, 4], P('tile'), may hold values from 0 to 3
- filter_stride_spread: int32 [4], replicated, may hold values from 1 to 4, as said below
Outputs:
- network_predicted_state: bfloat16 [2, 16, 64, 16, 128], P('ens', 'tile')
- state_input_derivative: float32 [2, 16, 64, 16, 128], P('ens', 'tile')
- initial_filter_derivative: float32 [9, 64, 64], replicated
- latter_filter_derivative: float32 [9, 128, 64], replicated
- penultimate_filter_derivative: float32 [9, 128, 128], replicated
- closing_filter_derivative: float32 [9, 64, 192], replicated
- initial_shift_derivative: float32 [64], replicated
- latter_shift_derivative: float32 [128], replicated
- penultimate_shift_derivative: float32 [128], replicated
- closing_shift_derivative: float32 [64], replicated
The draws below stay inside these ranges and needn't reach their ends.
Inputs may be any that keep to these rules, and one draw needn't show every extreme that they name: `codes`: bit 0 picks which of the two parallel edges of the sending tile is sent, bit 1 reverses it. `filter_stride_spread`: at least one layer has dilation 4 and one has dilation 1.
All inputs are finite; a program needn't handle non-finite values.
Results may differ from the reference program's by a relative error of at most 0.009.
Values may be sent and summed in bfloat16 or wider, within the bound.
No kernel may reach another device: no remote copies, remote signals or barrier semaphores. Data moves between devices by JAX's collectives and lax.ppermute only.
A program may use at most 128 MiB of HBM per device.

```python
import math
import jax
import jax.numpy as jnp
from jax import lax

C0 = 64
C1 = 128
H = 16
W = 128
LAYERS = 4
DMAX = 4
TILE_ROW = 8
MEMBERS = 2
TILES = 16


def draw_filter_stride_spread(key, part):
    key = jax.random.fold_in(key, 7)
    first_key, second_key = jax.random.split(key)
    values = jax.random.randint(first_key, (LAYERS,), 1, DMAX + 1)
    order = jax.random.permutation(second_key, LAYERS)
    positions = jnp.arange(LAYERS)
    values = jnp.where(positions == order[0], DMAX, values)
    values = jnp.where(positions == order[1], 1, values)
    return values.astype(jnp.int32)


def touch_ends(drawn, stream_key, smallest, top_value):
    shape = drawn.shape
    index_at = [jax.random.randint(jax.random.fold_in(stream_key, axis), (), 0, shape[axis]) for axis in range(len(shape))]
    drawn = drawn.at[tuple(index_at)].set(smallest)
    longest = shape.index(max(shape))
    index_at[longest] = (index_at[longest] + 1) % shape[longest]
    return drawn.at[tuple(index_at)].set(top_value)


def block_scale(rng, shape, pieces, smallest, top_value):
    level = 1.0
    for dim, parts in pieces:
        steps = jax.random.uniform(jax.random.fold_in(jax.random.fold_in(rng, 6), dim), (parts,), jnp.float32, smallest / len(pieces), top_value / len(pieces))
        level = level * jnp.repeat(jnp.exp(steps), shape[dim] // parts).reshape((-1,) + (1,) * (len(shape) - 1 - dim))
    return level


def normal_values(own_key, shape, spread, reach, pieces=(), kind=jnp.bfloat16):
    result = jax.random.normal(own_key, shape, jnp.float32) * spread
    if len(pieces) > 0:
        result = block_scale(own_key, shape, pieces, -0.22, 0.18) * result
    return jnp.clip(result, min=-reach, max=reach).astype(kind)


def setup_inputs(seed: int = 0) -> dict:
    key_list = jax.random.split(jax.random.key(seed), 13)
    return {
        "fields": normal_values(key_list[0], (MEMBERS, TILES, C0, H, W), 1.0, 6.0, ((0, 2), (1, 16))),
        "cotangent": normal_values(key_list[1], (MEMBERS, TILES, C0, H, W), 1.0, 6.0, ((0, 2), (1, 16))),
        "kernel_first": normal_values(key_list[2], (9, C0, C0), (9 * C0) ** -0.5, 0.25),
        "kernel_second": normal_values(key_list[3], (9, C1, C0), (9 * C0) ** -0.5, 0.25),
        "kernel_third": normal_values(key_list[4], (9, C1, C1), (9 * C1) ** -0.5, 0.1875),
        "closing_filter_weights": normal_values(key_list[5], (9, C0, C0 + C1), (9 * (C0 + C1)) ** -0.5, 0.15625),
        "offset_first": normal_values(key_list[6], (C0,), 0.5, 3.0, (), jnp.float32),
        "offset_second": normal_values(key_list[7], (C1,), 0.5, 3.0, (), jnp.float32),
        "offset_third": normal_values(key_list[8], (C1,), 0.5, 3.0, (), jnp.float32),
        "closing_shift_values": normal_values(key_list[9], (C0,), 0.5, 3.0, (), jnp.float32),
        "codes": touch_ends(jax.random.randint(key_list[10], (TILES, 4), 0, 4), jax.random.fold_in(key_list[10], 1), 0, 3).astype(jnp.int32),
        "filter_stride_spread": draw_filter_stride_spread(jax.random.fold_in(key_list[12], 71), 0),
    }


def exact_gelu(values):
    return jax.nn.gelu(values, approximate=False)

def gelu_slope(values):
    return jax.vjp(exact_gelu, values)[1](jnp.ones_like(values))[0]

def edge_columns(values, flag, margin):
    extent = values.shape[-1]
    picked = jnp.where(flag % 2 == 1, values[..., extent - margin:], values[..., :margin])
    return jnp.where(flag // 2 == 1, jnp.flip(picked, -2), picked)

def edge_rows(values, flag, margin):
    extent = values.shape[-2]
    picked = jnp.where(flag % 2 == 1, values[..., extent - margin:, :], values[..., :margin, :])
    return jnp.where(flag // 2 == 1, jnp.flip(picked, -1), picked)

def return_columns(summed, incoming, flag, margin):
    extent = summed.shape[-1]
    unflipped = jnp.where(flag // 2 == 1, jnp.flip(incoming, -2), incoming)
    nothing = jnp.zeros_like(unflipped)
    summed = summed.at[..., :margin].add(jnp.where(flag % 2 == 0, unflipped, nothing))
    return summed.at[..., extent - margin:].add(jnp.where(flag % 2 == 1, unflipped, nothing))

def return_rows(summed, incoming, flag, margin):
    extent = summed.shape[-2]
    unflipped = jnp.where(flag // 2 == 1, jnp.flip(incoming, -1), incoming)
    nothing = jnp.zeros_like(unflipped)
    summed = summed.at[..., :margin, :].add(jnp.where(flag % 2 == 0, unflipped, nothing))
    return summed.at[..., extent - margin:, :].add(jnp.where(flag % 2 == 1, unflipped, nothing))

def surround(values, codes, margin):
    column_fn = jax.vmap(edge_columns, in_axes=(0, 0, None))
    row_fn = jax.vmap(edge_rows, in_axes=(0, 0, None))
    toward_right = column_fn(values, codes[:, 3], margin)
    toward_left = column_fn(values, codes[:, 2], margin)
    leftward = jnp.roll(toward_right, 1, axis=0)
    rightward = jnp.roll(toward_left, -1, axis=0)
    widened = jnp.concatenate([leftward, values, rightward], axis=-1)
    toward_lower = row_fn(widened, codes[:, 1], margin)
    toward_upper = row_fn(widened, codes[:, 0], margin)
    upper_rim = jnp.roll(toward_lower, TILE_ROW, axis=0)
    lower_rim = jnp.roll(toward_upper, -TILE_ROW, axis=0)
    return jnp.concatenate([upper_rim, widened, lower_rim], axis=-2)

def fold_rims(padded, codes, margin):
    rows_all = padded.shape[-2]
    upper = padded[..., :margin, :]
    lower = padded[..., rows_all - margin:, :]
    inner = padded[..., margin:rows_all - margin, :]
    from_upper = jnp.roll(upper, -TILE_ROW, axis=0)
    from_lower = jnp.roll(lower, TILE_ROW, axis=0)
    rows_back = jax.vmap(return_rows, in_axes=(0, 0, 0, None))
    cols_back = jax.vmap(return_columns, in_axes=(0, 0, 0, None))
    inner = rows_back(inner, from_lower, codes[:, 0], margin)
    inner = rows_back(inner, from_upper, codes[:, 1], margin)
    cols_all = inner.shape[-1]
    left_part = inner[..., :margin]
    right_part = inner[..., cols_all - margin:]
    core = inner[..., margin:cols_all - margin]
    back_left = jnp.roll(left_part, -1, axis=0)
    back_right = jnp.roll(right_part, 1, axis=0)
    core = cols_back(core, back_right, codes[:, 2], margin)
    return cols_back(core, back_left, codes[:, 3], margin)

def product(first, second, form):
    return jnp.einsum(form, first.astype(jnp.float32), second.astype(jnp.float32), precision=lax.Precision.HIGHEST)

def start_of(row_tap, col_tap, spacing, border):
    zero = jnp.int32(0)
    return (zero, zero, border + (row_tap - 1) * spacing, border + (col_tap - 1) * spacing)

def convolve(padded, kernel, spacing, border):
    members, channels, rows_pad, cols_pad = padded.shape
    rows, cols = (rows_pad - 2 * border, cols_pad - 2 * border)
    summed = jnp.zeros((members, kernel.shape[1], rows, cols), jnp.float32)
    for row_tap in range(3):
        for col_tap in range(3):
            section = lax.dynamic_slice(padded, start_of(row_tap, col_tap, spacing, border), (members, channels, rows, cols))
            summed = summed + product(kernel[3 * row_tap + col_tap], section, 'oc,mchw->mohw')
    return summed

def kernel_terms(padded, grad, spacing, border):
    members, channels, rows_pad, cols_pad = padded.shape
    rows, cols = (rows_pad - 2 * border, cols_pad - 2 * border)
    listed = []
    for row_tap in range(3):
        for col_tap in range(3):
            section = lax.dynamic_slice(padded, start_of(row_tap, col_tap, spacing, border), (members, channels, rows, cols))
            listed.append(product(grad, section, 'mohw,mchw->oc'))
    return jnp.stack(listed)

def spread_back(grad, kernel, spacing, border):
    members, outs_count, rows, cols = grad.shape
    channels = kernel.shape[2]
    summed = jnp.zeros((members, channels, rows + 2 * border, cols + 2 * border), jnp.float32)
    for row_tap in range(3):
        for col_tap in range(3):
            begin = start_of(row_tap, col_tap, spacing, border)
            current = lax.dynamic_slice(summed, begin, (members, channels, rows, cols))
            summed = lax.dynamic_update_slice(summed, current + product(kernel[3 * row_tap + col_tap], grad, 'oc,mohw->mchw'), begin)
    return summed

def coarsen(values):
    lead = values.shape[:-2]
    rows, cols = (values.shape[-2], values.shape[-1])
    blocks = values.astype(jnp.float32).reshape(lead + (rows // 2, 2, cols // 2, 2))
    return lax.optimization_barrier(jnp.mean(blocks, axis=(-3, -1))).astype(jnp.bfloat16)

def refine(values):
    return jnp.repeat(jnp.repeat(values, 2, axis=-2), 2, axis=-1)

def collapse(values):
    lead = values.shape[:-2]
    rows, cols = (values.shape[-2], values.shape[-1])
    return lax.optimization_barrier(jnp.sum(values.reshape(lead + (rows // 2, 2, cols // 2, 2)), axis=(-3, -1)))

def reference(fields, cotangent, kernel_first, kernel_second, kernel_third, closing_filter_weights, offset_first, offset_second, offset_third, closing_shift_values, codes, filter_stride_spread):
    border = DMAX

    def apply_filters_throughout(padded, kernel, spacing):
        return lax.map(lambda single: convolve(single, kernel, spacing, border), padded)

    def terms_all(padded, grad, spacing):
        return lax.optimization_barrier(jnp.sum(lax.map(lambda pair: kernel_terms(pair[0], pair[1], spacing, border), (padded, grad)), axis=0))

    def back_all(grad, kernel, spacing):
        return fold_rims(lax.map(lambda single: spread_back(single, kernel, spacing, border), grad), codes, border)
    start_fields = jnp.swapaxes(fields, 0, 1)
    upstream = jnp.swapaxes(cotangent, 0, 1)
    first_pad = surround(start_fields, codes, border)
    first_pre = apply_filters_throughout(first_pad, kernel_first, filter_stride_spread[0]) + offset_first[:, None, None]
    first_act = exact_gelu(first_pre).astype(jnp.bfloat16)
    pooled = coarsen(first_act)
    second_pad = surround(pooled, codes, border)
    second_pre = apply_filters_throughout(second_pad, kernel_second, filter_stride_spread[1]) + offset_second[:, None, None]
    second_act = exact_gelu(second_pre).astype(jnp.bfloat16)
    third_pad = surround(second_act, codes, border)
    third_pre = apply_filters_throughout(third_pad, kernel_third, filter_stride_spread[2]) + offset_third[:, None, None]
    third_act = exact_gelu(third_pre).astype(jnp.bfloat16)
    joined = jnp.concatenate([refine(third_act), first_act], axis=-3)
    merged_halo_margin = surround(joined, codes, border)
    network_predicted_state = (apply_filters_throughout(merged_halo_margin, closing_filter_weights, filter_stride_spread[3]) + closing_shift_values[:, None, None]).astype(jnp.bfloat16)
    coarse_count = kernel_third.shape[1]
    joined_grad = back_all(upstream, closing_filter_weights, filter_stride_spread[3])
    third_delta = (collapse(joined_grad[..., :coarse_count, :, :]) * gelu_slope(third_pre)).astype(jnp.bfloat16)
    second_delta = (back_all(third_delta, kernel_third, filter_stride_spread[2]) * gelu_slope(second_pre)).astype(jnp.bfloat16)
    pooled_grad = back_all(second_delta, kernel_second, filter_stride_spread[1])
    first_grad = joined_grad[..., coarse_count:, :, :] + 0.25 * refine(pooled_grad)
    first_delta = (first_grad * gelu_slope(first_pre)).astype(jnp.bfloat16)
    state_input_derivative = back_all(first_delta, kernel_first, filter_stride_spread[0])
    scale = jnp.float32(1.0 / math.sqrt(MEMBERS * TILES * H * W))
    closing_filter_derivative = terms_all(merged_halo_margin, upstream, filter_stride_spread[3]) * scale
    penultimate_filter_derivative = terms_all(third_pad, third_delta, filter_stride_spread[2]) * scale
    latter_filter_derivative = terms_all(second_pad, second_delta, filter_stride_spread[1]) * scale
    initial_filter_derivative = terms_all(first_pad, first_delta, filter_stride_spread[0]) * scale
    axes_sum = (0, 1, 3, 4)
    initial_shift_derivative = lax.optimization_barrier(jnp.sum(first_delta.astype(jnp.float32), axis=axes_sum)) * scale
    latter_shift_derivative = lax.optimization_barrier(jnp.sum(second_delta.astype(jnp.float32), axis=axes_sum)) * scale
    penultimate_shift_derivative = lax.optimization_barrier(jnp.sum(third_delta.astype(jnp.float32), axis=axes_sum)) * scale
    closing_shift_derivative = lax.optimization_barrier(jnp.sum(upstream.astype(jnp.float32), axis=axes_sum)) * scale
    return (jnp.swapaxes(network_predicted_state, 0, 1), jnp.swapaxes(state_input_derivative, 0, 1), initial_filter_derivative, latter_filter_derivative, penultimate_filter_derivative, closing_filter_derivative, initial_shift_derivative, latter_shift_derivative, penultimate_shift_derivative, closing_shift_derivative)
```

```python
import functools
import math

import jax
import jax.numpy as jnp
from jax import lax
from jax.experimental import pallas as pl
from jax.experimental.pallas import tpu as pltpu
from jax.sharding import PartitionSpec as P

DMAX = 4
TILE_ROW = 8
LANES = 128
PITCH = 4
F32 = jnp.float32
BF16 = jnp.bfloat16


def lane_of(shape):
    return lax.broadcasted_iota(jnp.int32, shape, len(shape) - 1)


def turn(slab, by):
    if isinstance(by, int):
        by = by % LANES
        if by == 0:
            return slab
    else:
        by = jnp.bitwise_and(by, LANES - 1)
    return pltpu.roll(slab, by, axis=slab.ndim - 1)


def odd(code):
    return jnp.bitwise_and(code, 1)


def flipper(code, width):
    first = lax.broadcasted_iota(jnp.int32, (LANES, LANES), 0)
    second = lax.broadcasted_iota(jnp.int32, (LANES, LANES), 1)
    mirrored = jnp.bitwise_and(width - 1 - first, LANES - 1)
    target = jnp.where(code >= 2, mirrored, first)
    return jnp.where(second == target, 1.0, 0.0).astype(BF16)


def matmul(left, right):
    return jnp.dot(left, right, preferred_element_type=F32)


def matmul_t(left, right):
    return lax.dot_general(left, right, (((1,), (1,)), ((), ())), preferred_element_type=F32)


def halves(values):
    high = values.astype(BF16)
    return high, (values - high.astype(F32)).astype(BF16)


def pack_columns(row, count, first_lane, flip):
    packed = None
    for r in range(count):
        place = r if flip is None else jnp.where(flip, count - 1 - r, r)
        moved = turn(row(r), PITCH * place - first_lane)
        if packed is None:
            packed = moved
        else:
            packed = jnp.where(lane_of(moved.shape) // PITCH == place, moved, packed)
    return packed


def squeeze(packed, used):
    groups = LANES // used
    part = packed.shape[0] // groups
    lane = lane_of((part, LANES))
    whole = packed[:part]
    for g in range(1, groups):
        moved = turn(packed[g * part : (g + 1) * part], used * g)
        whole = jnp.where(lane // used == g, moved, whole)
    return whole


def expand(whole, used):
    groups = LANES // used
    return jnp.concatenate([turn(whole, -used * g) for g in range(groups)], axis=0)


def shorten(packed, count):
    if count <= 8:
        return packed
    return jnp.where(lane_of(packed.shape) < 16, packed, turn(packed, 32 - PITCH * count))


def short_base(code, count, margin):
    return odd(code) * (min(count, 8) - margin)


def units_of(channels, used):
    return channels * used // (LANES * 16)


def put_units(ref, index, at, whole):
    units = whole.shape[0] // 16
    shaped = whole.reshape(units, 16, LANES).astype(BF16)
    if index is None:
        ref[at : at + units] = shaped
    else:
        ref[index, at : at + units] = shaped


def get_units(ref, index, at, channels, used):
    units = units_of(channels, used)
    block = ref[at : at + units] if index is None else ref[index, at : at + units]
    return expand(block.reshape(units * 16, LANES), used)


def by_parity(sc, for_even, for_odd):
    return jnp.where(sc[10] == 0, for_even, for_odd)


def put_sides(refs, index, at, leftward, rightward, sc):
    put_units(refs[0], index, at, by_parity(sc, rightward, leftward))
    put_units(refs[1], index, at, by_parity(sc, leftward, rightward))


def get_sides(refs, index, at, channels, used, sc):
    first = get_units(refs[0], index, at, channels, used)
    second = get_units(refs[1], index, at, channels, used)
    return by_parity(sc, second, first), by_parity(sc, first, second)


def edge_messages(row, ref, sends, places, width, margin, sc):
    count = ref.shape[0]
    row_messages(ref, sends[0], places[0], width, margin, sc)
    packed = []
    for code in (sc[2], sc[3]):
        first_lane = jnp.where(odd(code) == 1, width - margin, 0)
        packed.append(pack_columns(row, count, first_lane, code >= 2))
    near = [squeeze(part, PITCH * count) for part in packed]
    put_sides(sends[1:3], None, places[1], near[0], near[1], sc)
    far = [squeeze(shorten(part, count), 32) for part in packed]
    for index in range(sends[3].shape[0]):
        put_sides(sends[3:5], index, places[2], far[0], far[1], sc)


def pass_on(extras, sends, places):
    for extra, out, at, dim in zip(extras, sends, (places[0],) + (places[1],) * 2 + (places[2],) * 2, (1, 0, 0, 1, 1)):
        size = extra.shape[dim]
        if dim == 0:
            out[at : at + size] = extra[...]
        else:
            for index in range(extra.shape[0]):
                out[index, at : at + size] = extra[index]


def pair_rows(rows, margin):
    half = margin // 2
    lane = lane_of(rows[0].shape)
    return [jnp.where(lane < 64, rows[k], turn(rows[k + half], 64)) for k in range(half)]


def row_messages(ref, out, at, width, margin, sc):
    count, channels = ref.shape[0], ref.shape[1]
    for side in range(2):
        base = jnp.where(odd(sc[side]) == 1, count - margin, 0)
        picked = ref[pl.ds(base, margin)].reshape(margin * channels, LANES).astype(BF16)
        turned = matmul(picked, flipper(sc[side], width)).reshape(margin, channels, LANES)
        store_rows(turned, out, side, at, width, margin)


def store_rows(turned, out, side, at, width, margin):
    channels = turned.shape[1]
    slabs = channels // out.shape[-2]
    rows = [turned[k].astype(BF16) for k in range(margin)]
    if width == 64:
        rows = pair_rows(rows, margin)
    for k, slab in enumerate(rows):
        out[side, at + k * slabs : at + (k + 1) * slabs] = slab.reshape(
            (slabs, channels // slabs, LANES)
        )


def load_row(ref, side, at, k, channels, width, margin):
    slabs = channels // ref.shape[-2]
    half = margin // 2
    index = k % half if width == 64 else k
    slab = ref[side, at + index * slabs : at + (index + 1) * slabs].reshape(channels, LANES)
    return turn(slab, 64) if width == 64 and k >= half else slab


def rim_sides(first, second, base, width, margin, code):
    lane = lane_of(first.shape)
    rows = []
    for k in range(margin):
        left = turn(first, LANES - margin - PITCH * (base + k))
        right = turn(second, width - PITCH * (base + k))
        rows.append(jnp.where(lane >= LANES - margin, left, right))
    channels = first.shape[0]
    flat = jnp.concatenate(rows, axis=0)
    turned = matmul(flat, flipper(code, width)).astype(BF16).reshape(margin, channels, LANES)
    return [turned[k] for k in range(margin)]


def padded_sides(received, places, count, channels, width, margin, sc):
    left, right = get_sides(received[1:3], None, places[1], channels, PITCH * count, sc)
    lane = lane_of((channels, LANES))
    rims = []
    for index, code in ((0, sc[4]), (received[3].shape[0] - 1, sc[5])):
        rims.append(
            rim_sides(
                *get_sides(received[3:5], index, places[2], channels, 32, sc),
                short_base(code, count, margin),
                width,
                margin,
                code,
            )
        )
    center = []
    for r in range(count):
        center.append(
            jnp.where(
                lane >= LANES - margin,
                turn(left, LANES - margin - PITCH * r),
                turn(right, width - PITCH * r),
            )
        )
    return rims[0] + center + rims[1]


def padded_rows(tile, received, places, width, margin, sc):
    rows_in = received[0]
    count, channels = tile.shape[0], tile.shape[1]
    sides = padded_sides(received, places, count, channels, width, margin, sc)
    lane = lane_of((channels, LANES))
    for r in range(count + 2 * margin):
        if r < margin:
            own = load_row(rows_in, 1, places[0], r, channels, width, margin)
        elif r < margin + count:
            own = tile[r - margin]
        else:
            own = load_row(rows_in, 0, places[0], r - margin - count, channels, width, margin)
        if width == 64:
            own = jnp.where(lane < width, own, sides[r])
        yield r, own, sides[r]


def store_shifts(taps, r, at, step, own, sides, width, spacing):
    channels = own.shape[0]
    lane = lane_of(own.shape)
    if width == 64:
        from_left, from_right = own, own
    else:
        from_left = jnp.where(lane >= LANES - spacing, sides, own)
        from_right = jnp.where(lane < spacing, sides, own)
    taps[r, at : at + channels] = turn(from_left, spacing)
    taps[r, step + at : step + at + channels] = own
    taps[r, 2 * step + at : 2 * step + at + channels] = turn(from_right, -spacing)


def fill_taps(taps, tile, received, places, width, sc, spacing):
    channels = tile.shape[1]
    for r, own, sides in padded_rows(tile, received, places, width, DMAX, sc):
        store_shifts(taps, r, 0, channels, own, sides, width, spacing)


def tap_pair(taps, i, spacing):
    sections = []
    for row in (i, i + 1):
        sections.append(
            jnp.concatenate([taps[row + DMAX + (a - 1) * spacing] for a in range(3)], axis=0)
        )
    return jnp.concatenate(sections, axis=1)


def column_of(offset):
    return jnp.concatenate([offset[...], offset[...]], axis=1)


def normal_cdf(values):
    return 0.5 + 0.5 * lax.erf(values * (2.0**-0.5))


def gelu(values):
    return values * normal_cdf(values)


def gelu_slope(values):
    density = jnp.exp(-0.5 * values * values) * (1.0 / math.sqrt(2.0 * math.pi))
    return normal_cdf(values) + values * density


def pool_matrix(weight):
    row = lax.broadcasted_iota(jnp.int32, (2 * LANES, LANES), 0)
    col = lax.broadcasted_iota(jnp.int32, (2 * LANES, LANES), 1)
    return jnp.where(jnp.bitwise_and(row, LANES - 1) // 2 == col, weight, 0.0).astype(BF16)


def side_pool_matrix():
    row = lax.broadcasted_iota(jnp.int32, (2 * LANES, LANES), 0)
    col = lax.broadcasted_iota(jnp.int32, (2 * LANES, LANES), 1)
    row = jnp.bitwise_and(row, LANES - 1)
    target = jnp.where(row >= 124, 126 + (row - 124) // 2, jnp.where(row < 4, 64 + row // 2, -1))
    return jnp.where(target == col, 1.0, 0.0).astype(BF16)


def spread_matrix():
    row = lax.broadcasted_iota(jnp.int32, (LANES, LANES), 0)
    col = lax.broadcasted_iota(jnp.int32, (LANES, LANES), 1)
    return jnp.where(col // 2 == row, 1.0, 0.0).astype(BF16)


def side_spread_matrix():
    row = lax.broadcasted_iota(jnp.int32, (LANES, LANES), 0)
    col = lax.broadcasted_iota(jnp.int32, (LANES, LANES), 1)
    source = jnp.where(col >= 124, 126 + (col - 124) // 2, jnp.where(col < 4, 64 + col // 2, -1))
    return jnp.where(source == row, 1.0, 0.0).astype(BF16)


def fill_delta(delta, rows):
    count = delta.shape[0] - 16
    nothing = jnp.zeros((8,) + delta.shape[1:], BF16)
    delta[0:8] = nothing
    delta[8 + count :] = nothing
    for r in range(count):
        delta[8 + r] = rows(r)


def spread_taps(delta, kernel, spacing, width):
    count = delta.shape[0] - 16
    channels = kernel.shape[0] // 3
    lane = lane_of((channels, LANES))
    for r in range(0, count + 2 * DMAX, 2):
        sections = []
        for row in (r, r + 1):
            sections.append(
                jnp.concatenate(
                    [delta[8 + row - DMAX - (a - 1) * spacing] for a in range(3)], axis=0
                )
            )
        both = matmul(kernel[...], jnp.concatenate(sections, axis=1))
        for k in range(2):
            part = both[:, k * LANES : (k + 1) * LANES]
            to_left = turn(part[:channels], -spacing)
            own = part[channels : 2 * channels]
            to_right = turn(part[2 * channels :], spacing)
            if width == 64:
                own = own + to_left + to_right
                yield r + k, own, own
            else:
                keep_right = lane >= spacing
                keep_left = lane < LANES - spacing
                own = own + jnp.where(keep_right, to_right, 0.0) + jnp.where(keep_left, to_left, 0.0)
                sides = jnp.where(keep_right, 0.0, to_right) + jnp.where(keep_left, 0.0, to_left)
                yield r + k, own, sides


def rim_messages(own, sides, sends, places, width, margin, sc):
    rows_out = sends[0]
    total, channels = own.shape[0], own.shape[1]
    count = total - 2 * margin
    lane = lane_of((channels, LANES))
    near = []
    for first_lane in (-margin, width):
        packed = pack_columns(lambda r: sides[margin + r].astype(BF16), count, first_lane, None)
        near.append(squeeze(packed, PITCH * count))
    put_sides(sends[1:3], None, places[1], near[0], near[1], sc)
    corners = []
    for side, code, start in ((0, sc[4], 0), (1, sc[5], margin + count)):
        mirror = flipper(code, width)
        flat = own[start : start + margin].reshape(margin * channels, LANES).astype(BF16)
        turned = matmul(flat, mirror).reshape(margin, channels, LANES)
        store_rows(turned, rows_out, side, places[0], width, margin)
        if width != 64:
            flat = sides[start : start + margin].reshape(margin * channels, LANES).astype(BF16)
            turned = matmul(flat, mirror).reshape(margin, channels, LANES)
        base = short_base(code, count, margin)
        left = jnp.zeros((channels, LANES), F32)
        right = jnp.zeros((channels, LANES), F32)
        for k in range(margin):
            here = lane // PITCH == base + k
            left = jnp.where(here, turn(turned[k], PITCH * (base + k) + margin), left)
            right = jnp.where(here, turn(turned[k], PITCH * (base + k) - width), right)
        corners.append((squeeze(left, 32), squeeze(right, 32)))
    if sends[3].shape[0] == 1:
        both = [corners[0][i] + corners[1][i] for i in range(2)]
        put_sides(sends[3:5], 0, places[2], both[0], both[1], sc)
    else:
        for index in range(2):
            left, right = corners[1 - index]
            put_sides(sends[3:5], index, places[2], left, right, sc)


def fold(total, inner, received, places, width, margin, sc):
    rows_in = received[0]
    count, channels = inner.shape[0], inner.shape[1]
    lane = lane_of((channels, LANES))
    used = PITCH * count
    found = [
        side.astype(F32)
        for side in get_sides(received[1:3], None, places[1], channels, used, sc)
    ]
    for index in range(received[3].shape[0]):
        for i, short in enumerate(get_sides(received[3:5], index, places[2], channels, 32, sc)):
            short = short.astype(F32)
            if count <= 8:
                found[i] = found[i] + jnp.where(lane < 32, short, 0.0)
            else:
                late = turn(short, used - 32)
                late = jnp.where((lane >= used - 16) & (lane < used), late, 0.0)
                found[i] = found[i] + jnp.where(lane < 16, short, late)
    for r in range(count):
        row = inner[r]
        for packed, code in ((found[0], sc[2]), (found[1], sc[3])):
            first = jnp.where(odd(code) == 1, width - margin, 0)
            place = jnp.where(code >= 2, count - 1 - r, r)
            moved = turn(packed, first - PITCH * place)
            row = row + jnp.where((lane >= first) & (lane < first + margin), moved, 0.0)
        total[r] = row
    for side, code in ((0, sc[1]), (1, sc[0])):
        base = odd(code) * (count - margin)
        for k in range(margin):
            total[base + k] = total[base + k] + load_row(
                rows_in, side, places[0], k, channels, width, margin
            ).astype(F32)


START = (0, 0, 0)
AFTER_POOLED = (2, 1, 1)
AFTER_SECOND = (4, 2, 2)


def weights_kernel(swapped, *refs):
    kernels, arrived = refs[20:24], refs[24]
    copies = [pltpu.make_async_copy(refs[i], kernels[i], arrived.at[i]) for i in range(4)]
    for copy in copies:
        copy.start()
    for i, (kernel, offset) in enumerate(zip(kernels, refs[4:8])):
        forward, backward, shift = refs[8 + i], refs[12 + i], refs[16 + i]
        copies[i].wait()
        outs, channels = kernel.shape[1:]
        if swapped[i]:
            outs, channels = channels, outs
        for tap in range(9):
            a, e = tap // 3, tap % 3
            own = kernel[tap]
            across = jnp.transpose(own.astype(F32)).astype(BF16)
            if swapped[i]:
                own, across = across, own
            forward[:, tap * channels : (tap + 1) * channels] = own
            backward[e * channels : (e + 1) * channels, a * outs : (a + 1) * outs] = across
        row = lax.broadcasted_iota(jnp.int32, (outs, outs), 0)
        col = lax.broadcasted_iota(jnp.int32, (outs, outs), 1)
        column = jnp.sum(jnp.where(row == col, offset[...], 0.0), axis=1, keepdims=True)
        shift[...] = jnp.broadcast_to(column, shift.shape)


def fields_kernel(sc, fields, tile, *sends):
    tile[...] = jnp.swapaxes(fields[...], 0, 1)
    edge_messages(lambda r: tile[r], tile, sends, START, LANES, DMAX, sc)
    last, shape = sends[0].shape[1] - 1, sends[0].shape[2:]
    for side in range(2):
        code = sc[side].astype(F32)
        sends[0][side, last] = jnp.broadcast_to(code, shape).astype(BF16)


def first_kernel(own_sc, tile, *refs):
    received, (kernel, offset) = refs[:5], refs[5:7]
    act_out, pre_out, pooled_out, sc, taps = refs[7:12]
    sends = refs[12:]
    last = received[0].shape[1] - 1
    for i in range(13):
        sc[i] = own_sc[i]
    for i in range(2):
        sc[4 + i] = jnp.max(received[0][1 - i, last].astype(F32)).astype(jnp.int32)
    spacing = own_sc[6]
    fill_taps(taps, tile, received, START, LANES, sc, spacing)
    pool = pool_matrix(0.25)
    shift = column_of(offset)
    for i in range(0, tile.shape[0], 2):
        pre = matmul(kernel[...], tap_pair(taps, i, spacing)) + shift
        act = gelu(pre).astype(BF16)
        for k in range(2):
            act_out[i + k] = act[:, k * LANES : (k + 1) * LANES]
            pre_out[i + k] = pre[:, k * LANES : (k + 1) * LANES]
        pooled_out[i // 2] = matmul(act, pool).astype(BF16)
    edge_messages(
        lambda r: pooled_out[r], pooled_out, sends, START, 64, DMAX, sc
    )
    edge_messages(
        lambda r: act_out[r], act_out, sends, AFTER_POOLED, LANES, DMAX, sc
    )


def second_kernel(sc, tile, *refs):
    received, (kernel, offset), extras = refs[:5], refs[5:7], refs[7:12]
    act_out, pre_out, taps = refs[12:15]
    sends = refs[15:]
    spacing = sc[7]
    fill_taps(taps, tile, received, START, 64, sc, spacing)
    shift = column_of(offset)
    for i in range(0, tile.shape[0], 2):
        pre = matmul(kernel[...], tap_pair(taps, i, spacing)) + shift
        both = beside(pre[:, :LANES], pre[:, LANES:])
        act = gelu(both).astype(BF16)
        for k in range(2):
            act_out[i + k] = turn(act, 64 * k)
        pre_out[i // 2] = both
    edge_messages(lambda r: act_out[r], act_out, sends, START, 64, DMAX, sc)
    pass_on(extras, sends, AFTER_SECOND)


def slopes_kernel(*refs):
    half = len(refs) // 2
    for values, out in zip(refs[:half], refs[half:]):
        for r in range(values.shape[0]):
            out[r] = gelu_slope(values[r])


def beside(first, second):
    return jnp.where(lane_of(first.shape) < 64, first, turn(second, 64))


def masked(values, width):
    return jnp.where(lane_of(values.shape) < width, values, jnp.zeros_like(values))


def back_part(sc, delta, kernel, spacing, width, inner_out, sends, own_all, sides_all):
    count = delta.shape[0] - 16
    for r, own, sides in spread_taps(delta, kernel, spacing, width):
        own_all[r] = own
        if width != 64:
            sides_all[r] = sides
    for r in range(count):
        inner_out[r] = own_all[DMAX + r]
    rim_messages(own_all, sides_all, sends, START, width, DMAX, sc)


def third_kernel(sc, tile, *refs):
    received, (kernel, offset, coarse, back) = refs[:5], refs[5:9]
    act_out, delta_out, inner_out = refs[9:12]
    sends, (taps, delta, own_all, coarse_sum) = refs[12:17], refs[17:]
    fold(coarse_sum, coarse, received, AFTER_SECOND, 64, 2, sc)
    spacing = sc[8]
    fill_taps(taps, tile, received, START, 64, sc, spacing)
    shift = column_of(offset)
    for i in range(0, tile.shape[0], 2):
        pre = matmul(kernel[...], tap_pair(taps, i, spacing)) + shift
        both = beside(pre[:, :LANES], pre[:, LANES:])
        act = gelu(both).astype(BF16)
        change = (beside(coarse_sum[i], coarse_sum[i + 1]) * gelu_slope(both)).astype(BF16)
        for k in range(2):
            act_out[i + k] = turn(act, 64 * k)
            delta_out[i + k] = masked(turn(change, 64 * k), 64)
    fill_delta(delta, lambda r: delta_out[r])
    back_part(sc, delta, back, spacing, 64, inner_out, sends, own_all, own_all)
    edge_messages(lambda r: act_out[r], act_out, sends, AFTER_SECOND, 64, 2, sc)


def middle_kernel(sc, inner, *refs):
    received, (slope, back), extras = refs[:5], refs[5:7], refs[7:12]
    delta_out, inner_out = refs[12:14]
    sends, (total, delta, own_all) = refs[14:19], refs[19:]
    fold(total, inner, received, START, 64, DMAX, sc)
    for r in range(0, inner.shape[0], 2):
        change = (beside(total[r], total[r + 1]) * slope[r // 2]).astype(BF16)
        for k in range(2):
            delta_out[r + k] = masked(turn(change, 64 * k), 64)
    fill_delta(delta, lambda r: delta_out[r])
    back_part(sc, delta, back, sc[7], 64, inner_out, sends, own_all, own_all)
    pass_on(extras, sends, AFTER_POOLED)


def lower_kernel(sc, inner, *refs):
    received, (slope, skip_inner, back) = refs[:5], refs[5:8]
    delta_out, inner_out = refs[8:10]
    sends, (total, skip, delta, own_all, sides_all) = refs[10:15], refs[15:]
    fold(total, inner, received, START, 64, DMAX, sc)
    fold(skip, skip_inner, received, AFTER_POOLED, LANES, DMAX, sc)
    spread = spread_matrix()
    for r in range(inner.shape[0]):
        lane = lane_of(total[r].shape)
        high, low = halves(jnp.where(lane < 64, total[r], 0.0))
        wide = 0.25 * (matmul(high, spread) + matmul(low, spread))
        for k in range(2):
            row = 2 * r + k
            delta_out[row] = ((skip[row] + wide) * slope[row]).astype(BF16)
    fill_delta(delta, lambda r: delta_out[r])
    back_part(sc, delta, back, sc[6], LANES, inner_out, sends, own_all, sides_all)


def last_kernel(sc, inner, *refs):
    received, out, total = refs[:5], refs[5], refs[6]
    fold(total, inner, received, START, LANES, DMAX, sc)
    out[...] = jnp.swapaxes(total[...], 0, 1)


def upstream_kernel(sc, cotangent, back, *refs):
    upstream, coarse_out, skip_out = refs[:3]
    coarse_sends, skip_sends = refs[3:8], refs[8:13]
    delta, own_all, sides_all, coarse_all = refs[13:]
    upstream[...] = jnp.swapaxes(cotangent[...], 0, 1)
    fill_delta(delta, lambda r: upstream[r])
    pool = jnp.concatenate([pool_matrix(1.0), side_pool_matrix()], axis=0)
    pending = None
    for r, own, sides in spread_taps(delta, back, sc[9], LANES):
        own_all[r] = own[128:]
        sides_all[r] = sides[128:]
        if pending is None:
            pending = (own[:128], sides[:128])
        else:
            high, low = halves(
                jnp.concatenate([pending[0], own[:128], pending[1], sides[:128]], axis=1)
            )
            coarse_all[r // 2] = matmul(high, pool) + matmul(low, pool)
            pending = None
    for r in range(coarse_out.shape[0]):
        coarse_out[r] = coarse_all[2 + r]
    for r in range(skip_out.shape[0]):
        skip_out[r] = own_all[4 + r]
    rim_messages(coarse_all, coarse_all, coarse_sends, START, 64, 2, sc)
    rim_messages(own_all, sides_all, skip_sends, START, LANES, 4, sc)


def put_terms(out, at, sums, sides):
    outs, columns = sums.shape
    whole = columns // LANES
    for k in range(whole):
        out[at + k * outs : at + (k + 1) * outs] = sums[:, k * LANES : (k + 1) * LANES].astype(BF16)
    if columns % LANES:
        wide = jnp.concatenate(
            [jnp.broadcast_to(side, (outs, 64 // len(sides))) for side in sides], axis=1
        )
        tail = jnp.concatenate([sums[:, whole * LANES :], wide], axis=1)
        out[at + whole * outs : at + (whole + 1) * outs] = tail.astype(BF16)


def row_sum(rows):
    total = None
    for r in range(rows.shape[0]):
        row = rows[r].astype(F32)
        total = row if total is None else total + row
    return jnp.sum(total, axis=1, keepdims=True)


def layer_terms(taps, delta, spacing, use=None):
    sums = None
    for i in range(0, delta.shape[0], 2):
        section = tap_pair(taps, i, spacing)
        if use is not None:
            use(i, section)
        part = matmul_t(jnp.concatenate([delta[i], delta[i + 1]], axis=1), section)
        sums = part if sums is None else sums + part
    return sums


def third_terms_kernel(sc, second, delta, *refs):
    third_in, (out, taps) = refs[:5], refs[5:]
    fill_taps(taps, second, third_in, START, 64, sc, sc[8])
    put_terms(out, 0, layer_terms(taps, delta, sc[8]), None)


def joined_kernel(
    sc, coarse, fine, taps_second, delta_third, delta_second, upstream, kernel, offset, *refs
):
    second_in, back_in = refs[:5], refs[5:10]
    state_out, out, taps, state_all = refs[10:]
    sums = layer_terms(taps_second, delta_second, sc[7])
    put_terms(out, 0, sums, [row_sum(delta_second), row_sum(delta_third)])
    after = -(-sums.shape[1] // LANES) * sums.shape[0]
    spacing = sc[9]
    spread = jnp.concatenate([spread_matrix(), side_spread_matrix()], axis=1)
    for r, own, _ in padded_rows(coarse, back_in, AFTER_SECOND, 64, 2, sc):
        wide = matmul(own, spread).astype(BF16)
        for k in range(2):
            store_shifts(
                taps, 2 * r + k, 0, 192, wide[:, :LANES], wide[:, LANES:], LANES, spacing
            )
    for r, own, sides in padded_rows(fine, second_in, AFTER_POOLED, LANES, 4, sc):
        store_shifts(taps, r, 128, 192, own, sides, LANES, spacing)
    shift = column_of(offset)

    def use(i, section):
        state = (matmul(kernel[...], section) + shift).astype(BF16)
        for k in range(2):
            state_all[i + k] = state[:, k * LANES : (k + 1) * LANES]

    put_terms(out, after, layer_terms(taps, upstream, spacing, use), [row_sum(upstream)])
    state_out[...] = jnp.swapaxes(state_all[...], 0, 1)


def first_terms_kernel(sc, taps, delta, third_terms, terms, give, keep, whole):
    rows = 0
    for part in (third_terms, terms):
        whole[rows : rows + part.shape[0]] = part[...]
        rows += part.shape[0]
    sums = layer_terms(taps, delta, sc[6])
    put_terms(whole, rows, sums, [row_sum(delta)])
    rows += -(-sums.shape[1] // LANES) * sums.shape[0]
    whole[rows:] = jnp.zeros((whole.shape[0] - rows, LANES), BF16)
    half = keep.shape[0]
    keep[...] = whole[pl.ds(pl.multiple_of(sc[10] * half, 16), half)]
    give[...] = whole[pl.ds(pl.multiple_of((1 - sc[10]) * half, 16), half)]


def core_sum_kernel(sc, keep, given, own, *gives):
    size = own.shape[0]
    for i, out in enumerate((own,) + gives):
        member = sc[11] if i < 2 else 1 - sc[11]
        chip = sc[12] if i % 2 == 0 else 1 - sc[12]
        rows = pl.ds(pl.multiple_of((2 * member + chip) * size, 16), size)
        out[...] = (keep[rows].astype(F32) + given[rows].astype(F32)).astype(out.dtype)


def adding_kernel(*refs):
    total = refs[0][...].astype(F32)
    for ref in refs[1:-1]:
        total = total + ref[...].astype(F32)
    refs[-1][...] = total.astype(BF16)


def unpack_kernel(scale, layouts, biases, sc, *refs):
    eighths, outs, summed = refs[:8], refs[8:-1], refs[-1]
    size = eighths[0].shape[0]
    for i, eighth in enumerate(eighths):
        bits = [sc[10 + k] if (i >> (2 - k)) % 2 == 0 else 1 - sc[10 + k] for k in range(3)]
        at = pl.multiple_of((4 * bits[0] + 2 * bits[1] + bits[2]) * size, 16)
        summed[pl.ds(at, size)] = eighth[...]
    for (start, outs_count, channels, swapped), out in zip(layouts, outs):
        def slab_at(slab):
            first = start + slab * outs_count
            return summed[first : first + outs_count].astype(F32) * scale

        if swapped:
            for slab in range(5):
                across = jnp.transpose(slab_at(slab))
                for tap in range(2 * slab, min(2 * slab + 2, 9)):
                    at = (tap - 2 * slab) * channels
                    out[tap] = across[at : at + channels]
            continue
        for tap in range(9):
            first, last = tap * channels, (tap + 1) * channels
            found = []
            while first < last:
                slab = first // LANES
                end = min(last, (slab + 1) * LANES)
                found.append(slab_at(slab)[:, first - slab * LANES : end - slab * LANES])
                first = end
            out[tap] = found[0] if len(found) == 1 else jnp.concatenate(found, axis=1)
    for (start, count, lane), out in zip(biases, outs[len(layouts) :]):
        block = summed[start : start + count].astype(F32)
        column = jnp.sum(
            jnp.where(lane_of(block.shape) == lane, block, 0.0), axis=1, keepdims=True
        )
        row = lax.broadcasted_iota(jnp.int32, (count, count), 0)
        col = lax.broadcasted_iota(jnp.int32, (count, count), 1)
        out[...] = jnp.sum(jnp.where(row == col, column, 0.0), axis=0, keepdims=True) * scale


def call(body, inputs, outputs, scratch=(), flops=0, scalars=1, copied=0, name=None):
    specs = [pl.BlockSpec(memory_space=pltpu.VMEM)] * len(inputs)
    specs[:copied] = [pl.BlockSpec(memory_space=pl.ANY)] * copied
    arrived = [pltpu.SemaphoreType.DMA((copied,))] if copied else []
    for i in range(scalars):
        specs[i] = pl.BlockSpec(memory_space=pltpu.SMEM)
    moved = sum(math.prod(shape) * jnp.dtype(kind).itemsize for shape, kind in outputs)
    moved += sum(array.size * array.dtype.itemsize for array in inputs)
    spaces = [pltpu.SMEM if kind == jnp.int32 else pltpu.VMEM for _, kind in outputs]
    return pl.pallas_call(
        body,
        out_shape=[jax.ShapeDtypeStruct(shape, kind) for shape, kind in outputs],
        in_specs=specs,
        out_specs=[pl.BlockSpec(memory_space=space) for space in spaces],
        scratch_shapes=[pltpu.VMEM(shape, kind) for shape, kind in scratch] + arrived,
        compiler_params=pltpu.CompilerParams(vmem_limit_bytes=24 * 1024 * 1024),
        cost_estimate=pl.CostEstimate(flops=flops, bytes_accessed=moved, transcendentals=0),
        name=name,
    )(*inputs)


def shifted(array, for_even, for_odd):
    devices = lax.axis_size("tile")
    pairs = [(i, (i + (for_odd if i % 2 else for_even)) % devices) for i in range(devices)]
    return lax.ppermute(array, "tile", pairs)


def wrapped():
    return lax.axis_size("tile") == 2 * TILE_ROW


def other_tile(array, bit):
    pairs = [(i, i ^ (1 << bit)) for i in range(lax.axis_size("tile"))]
    return lax.ppermute(array, "tile", pairs)


def other_member(array):
    return lax.ppermute(array, "ens", [(0, 1), (1, 0)])


def other_both(array, bit):
    tiles = lax.axis_size("tile")
    pairs = [(i, (i ^ (1 << bit)) + tiles if i < tiles else (i ^ (1 << bit)) - tiles)
             for i in range(2 * tiles)]
    return lax.ppermute(array, ("ens", "tile"), pairs)


def exchange_rows(rows):
    if wrapped():
        return shifted(rows, TILE_ROW, TILE_ROW)
    return jnp.stack(
        [shifted(rows[0], -TILE_ROW, -TILE_ROW), shifted(rows[1], TILE_ROW, TILE_ROW)]
    )


def exchange(rows, near_a, near_b, far_a, far_b):
    row = TILE_ROW
    rows_in = exchange_rows(rows)
    if wrapped():
        a_in = shifted(far_a, row + 1, row - 1)
        b_in = shifted(far_b, row - 1, row + 1)
    else:
        a_in = jnp.stack(
            [shifted(far_a[0], row + 1, row - 1), shifted(far_a[1], 1 - row, -1 - row)]
        )
        b_in = jnp.stack(
            [shifted(far_b[0], row - 1, row + 1), shifted(far_b[1], -1 - row, 1 - row)]
        )
    return [rows_in, shifted(near_a, 1, -1), shifted(near_b, -1, 1), a_in, b_in]


def shards(
    fields,
    cotangent,
    kernel_first,
    kernel_second,
    kernel_third,
    closing_filter_weights,
    offset_first,
    offset_second,
    offset_third,
    closing_shift_values,
    codes,
    filter_stride_spread,
):
    members, _, low, height, width = fields.shape
    high = kernel_third.shape[1]
    half = height // 2
    fars = 1 if wrapped() else 2
    tile_index = lax.axis_index("tile")
    place = [tile_index & 1, lax.axis_index("ens") & 1, (tile_index >> 1) & 1]
    own_sc = jnp.concatenate(
        [codes[0], jnp.zeros((2,), jnp.int32), filter_stride_spread]
        + [bit.astype(jnp.int32)[None] for bit in place]
    )

    def sends(rows, near, far):
        return (
            [((2, rows, 64, LANES), BF16)]
            + [((near, 16, LANES), BF16)] * 2
            + [((fars, far, 16, LANES), BF16)] * 2
        )

    fine_tile = ((height, low, LANES), BF16)
    fine_grad = ((height, low, LANES), F32)
    tile, *sent = call(
        fields_kernel,
        [own_sc, fields[0, 0]],
        [fine_tile, ((2, DMAX * low // 16 + 1, 16, LANES), BF16)] + sends(5, 2, 1)[1:],
        name="fields_edges",
    )
    first_in = exchange(*sent)

    weights = [kernel_first, kernel_second, kernel_third, closing_filter_weights]
    offsets = [offset_first, offset_second, offset_third, closing_shift_values]
    swapped = [k.shape[1] % LANES == 0 and k.shape[2] % LANES != 0 for k in weights]
    forms = call(
        functools.partial(weights_kernel, swapped),
        [jnp.swapaxes(k, 1, 2) if swap else k for k, swap in zip(weights, swapped)]
        + [offset[None] for offset in offsets],
        scratch=[
            ((9, k.shape[2], k.shape[1]) if swap else k.shape, BF16)
            for k, swap in zip(weights, swapped)
        ],
        copied=4,
        outputs=        [((k.shape[1], 9 * k.shape[2]), BF16) for k in weights]
        + [((3 * k.shape[2], 3 * k.shape[1]), BF16) for k in weights]
        + [((k.shape[1], LANES), F32) for k in weights],
        scalars=0,
        name="weights",
    )
    forward, backward, shifts = forms[:4], forms[4:8], forms[8:]

    first_taps = ((height + 8, 3 * low, LANES), BF16)
    act_first, pre_first, pooled, sc, taps_first, *sent = call(
        first_kernel,
        [own_sc, tile, *first_in, forward[0], shifts[0]],
        [fine_tile, fine_grad, ((half, low, LANES), BF16), ((13,), jnp.int32), first_taps]
        + sends(6, 3, 2),
        flops=2 * 9 * low * low * height * width,
        name="first_layer",
    )
    second_in = exchange(*sent)

    upstream, coarse_inner, skip_inner, *rims = call(
        upstream_kernel,
        [sc, cotangent[0, 0], backward[3]],
        [fine_tile, ((half, high, LANES), F32), fine_grad] + sends(2, 2, 2) + sends(4, 2, 1),
        [
            ((height + 16, low, LANES), BF16),
            ((height + 8, low, LANES), F32),
            ((height + 8, low, LANES), F32),
            ((half + 4, high, LANES), F32),
        ],
        flops=2 * 9 * low * (low + high) * height * width,
        name="cotangent_back",
    )
    coarse_rims, skip_rims = rims[:5], rims[5:]

    second_taps = ((half + 8, 3 * low, LANES), BF16)
    act_second, pre_second, taps_second, *sent = call(
        second_kernel,
        [sc, pooled, *second_in, forward[1], shifts[1], *coarse_rims],
        [((half, high, LANES), BF16), ((half // 2, high, LANES), F32), second_taps]
        + sends(6, 4, 4),
        flops=2 * 9 * low * high * half * LANES,
        name="second_layer",
    )
    third_in = exchange(*sent)
    slope_first, slope_second = call(
        slopes_kernel,
        [pre_first, pre_second],
        [fine_grad, ((half // 2, high, LANES), F32)],
        scalars=0,
        name="slopes",
    )
    coarse_inner, slope_first = lax.optimization_barrier((coarse_inner, slope_first))

    third_taps = ((half + 8, 3 * high, LANES), BF16)
    act_third, delta_third, inner, *sent = call(
        third_kernel,
        [sc, act_second, *third_in, forward[2], shifts[2], coarse_inner, backward[2]],
        [((half, high, LANES), BF16)] * 2 + [((half, high, LANES), F32)] + sends(6, 4, 4),
        [
            third_taps,
            ((half + 16, high, LANES), BF16),
            ((half + 8, high, LANES), F32),
            ((half, high, LANES), F32),
        ],
        flops=2 * 2 * 9 * high * high * half * LANES,
        name="third_layer_and_back",
    )
    back_in = exchange(*sent)
    (third_terms,) = call(
        third_terms_kernel,
        [sc, act_second, delta_third, *third_in],
        [((9 * high, LANES), BF16)],
        [third_taps],
        flops=2 * 9 * high * high * half * LANES,
        name="third_terms",
    )
    inner, third_terms = lax.optimization_barrier((inner, third_terms))

    delta_second, inner, *sent = call(
        middle_kernel,
        [sc, inner, *back_in, slope_second, backward[1], *skip_rims],
        [((half, high, LANES), BF16), ((half, low, LANES), F32)] + sends(6, 3, 2),
        [
            ((half, high, LANES), F32),
            ((half + 16, high, LANES), BF16),
            ((half + 8, low, LANES), F32),
        ],
        flops=2 * 9 * low * high * half * LANES,
        name="second_back",
    )
    lower_in = exchange(*sent)

    narrow = -(-9 * low // LANES)
    wide = -(-9 * (low + high) // LANES)
    upper_rows = narrow * high + wide * low
    state, upper_terms = call(
        joined_kernel,
        [
            sc, act_third, act_first, taps_second, delta_third, delta_second, upstream, forward[3],
            shifts[3], *second_in, *back_in,
        ],
        [((low, height, LANES), BF16), ((upper_rows, LANES), BF16)],
        [
            ((height + 8, 3 * (low + high), LANES), BF16),
            fine_tile,
        ],
        flops=2 * 2 * 9 * low * (low + high) * height * width,
        name="joined_layer_and_terms",
    )
    lower_in[0], upper_terms = lax.optimization_barrier((lower_in[0], upper_terms))

    delta_first, inner, *sent = call(
        lower_kernel,
        [sc, inner, *lower_in, slope_first, skip_inner, backward[0]],
        [fine_tile, fine_grad] + sends(4, 2, 1),
        [
            ((half, low, LANES), F32),
            fine_grad,
            ((height + 16, low, LANES), BF16),
            ((height + 8, low, LANES), F32),
            ((height + 8, low, LANES), F32),
        ],
        flops=2 * 9 * low * low * height * width,
        name="first_back",
    )

    tiles = lax.axis_size("tile")
    rows = 9 * high + upper_rows + narrow * low
    size = -(-rows // (8 * 16)) * 16

    def part(count):
        return ((count * size, LANES), BF16)

    give, keep = call(
        first_terms_kernel,
        [sc, taps_first, delta_first, third_terms, upper_terms],
        [part(4)] * 2,
        [part(8)],
        flops=2 * 9 * low * low * height * width,
        name="first_terms",
    )
    given = other_tile(give, 0)
    own, *gives = call(
        core_sum_kernel,
        [sc, keep, given],
        [((size, LANES), F32)] + [part(1)] * 3,
        name="core_sum",
    )
    given = [other_tile(gives[0], 1), other_member(gives[1]), other_both(gives[2], 1)]
    last_in = exchange(*sent)
    (total,) = call(adding_kernel, [own, *given], [part(1)], scalars=0, name="chip_sum")
    last_bit = tiles.bit_length() - 2
    for bit in range(2, last_bit + 1):
        if bit == last_bit:
            total, *last_in = lax.optimization_barrier((total, *last_in))
        given = other_tile(total, bit)
        (total,) = call(adding_kernel, [total, given], [part(1)], scalars=0, name=f"sum_{bit}")
    (derivative,) = call(
        last_kernel,
        [sc, inner, *last_in],
        [((low, height, LANES), F32)],
        [fine_grad],
        name="last_fold",
    )

    total, derivative = lax.optimization_barrier((total, derivative))
    eighths = [total, other_tile(total, 1), other_member(total), other_both(total, 1)]
    eighths = eighths + [other_tile(eighth, 0) for eighth in eighths]

    all_tiles = members * lax.axis_size("ens") * lax.axis_size("tile")
    scale = 1.0 / math.sqrt(all_tiles * height * width)
    upper_rows += 9 * high
    starts = [upper_rows, 9 * high, 0, upper_rows - wide * low]
    layouts = [
        (start, k.shape[1], k.shape[2], swap) for start, k, swap in zip(starts, weights, swapped)
    ]
    tail = 9 * high + (narrow - 1) * high
    biases = [(rows - low, low, 64), (tail, high, 64), (tail, high, 96), (upper_rows - low, low, 64)]
    grads = call(
        functools.partial(unpack_kernel, scale, layouts, biases),
        [sc, *eighths],
        [
            ((9, channels, outs) if swap else (9, outs, channels), F32)
            for _, outs, channels, swap in layouts
        ]
        + [((1, count), F32) for _, count, _ in biases],
        [part(8)],
        name="unpack_sums",
    )
    return (
        state[None, None],
        derivative[None, None],
        *[jnp.swapaxes(g, 1, 2) if swap else g for g, swap in zip(grads[:4], swapped)],
        *[grad[0] for grad in grads[4:]],
    )


def solution(mesh):
    tiles = P("ens", "tile", None, None, None)
    in_specs = (tiles, tiles) + (P(),) * 8 + (P("tile", None), P())
    out_specs = (tiles, tiles) + (P(),) * 8
    return jax.shard_map(shards, mesh=mesh, in_specs=in_specs, out_specs=out_specs, check_vma=False)
```

```python
import functools
import math

import jax
import jax.numpy as jnp
from jax import lax
from jax.experimental import pallas as pl
from jax.experimental.pallas import tpu as pltpu
from jax.sharding import PartitionSpec as P

DMAX = 4
TILE_ROW = 8
LANES = 128
PITCH = 4
F32 = jnp.float32
BF16 = jnp.bfloat16


def lane_of(shape):
    return lax.broadcasted_iota(jnp.int32, shape, len(shape) - 1)


def turn(slab, by):
    if isinstance(by, int):
        by = by % LANES
        if by == 0:
            return slab
    else:
        by = jnp.bitwise_and(by, LANES - 1)
    return pltpu.roll(slab, by, axis=slab.ndim - 1)


def odd(code):
    return jnp.bitwise_and(code, 1)


def flipper(code, width):
    first = lax.broadcasted_iota(jnp.int32, (LANES, LANES), 0)
    second = lax.broadcasted_iota(jnp.int32, (LANES, LANES), 1)
    mirrored = jnp.bitwise_and(width - 1 - first, LANES - 1)
    target = jnp.where(code >= 2, mirrored, first)
    return jnp.where(second == target, 1.0, 0.0).astype(BF16)


def matmul(left, right):
    return jnp.dot(left, right, preferred_element_type=F32)


def matmul_t(left, right):
    return lax.dot_general(left, right, (((1,), (1,)), ((), ())), preferred_element_type=F32)


def halves(values):
    high = values.astype(BF16)
    return high, (values - high.astype(F32)).astype(BF16)


def pack_columns(row, count, first_lane, flip):
    packed = None
    for r in range(count):
        place = r if flip is None else jnp.where(flip, count - 1 - r, r)
        moved = turn(row(r), PITCH * place - first_lane)
        if packed is None:
            packed = moved
        else:
            packed = jnp.where(lane_of(moved.shape) // PITCH == place, moved, packed)
    return packed


def squeeze(packed, used):
    groups = LANES // used
    part = packed.shape[0] // groups
    lane = lane_of((part, LANES))
    whole = packed[:part]
    for g in range(1, groups):
        moved = turn(packed[g * part : (g + 1) * part], used * g)
        whole = jnp.where(lane // used == g, moved, whole)
    return whole


def expand(whole, used):
    groups = LANES // used
    return jnp.concatenate([turn(whole, -used * g) for g in range(groups)], axis=0)


def shorten(packed, count):
    if count <= 8:
        return packed
    return jnp.where(lane_of(packed.shape) < 16, packed, turn(packed, 32 - PITCH * count))


def short_base(code, count, margin):
    return odd(code) * (min(count, 8) - margin)


def units_of(channels, used):
    return channels * used // (LANES * 16)


def put_units(ref, index, at, whole):
    units = whole.shape[0] // 16
    shaped = whole.reshape(units, 16, LANES).astype(BF16)
    if index is None:
        ref[at : at + units] = shaped
    else:
        ref[index, at : at + units] = shaped


def get_units(ref, index, at, channels, used):
    units = units_of(channels, used)
    block = ref[at : at + units] if index is None else ref[index, at : at + units]
    return expand(block.reshape(units * 16, LANES), used)


def by_parity(sc, for_even, for_odd):
    return jnp.where(sc[10] == 0, for_even, for_odd)


def put_sides(refs, index, at, leftward, rightward, sc):
    put_units(refs[0], index, at, by_parity(sc, rightward, leftward))
    put_units(refs[1], index, at, by_parity(sc, leftward, rightward))


def get_sides(refs, index, at, channels, used, sc):
    first = get_units(refs[0], index, at, channels, used)
    second = get_units(refs[1], index, at, channels, used)
    return by_parity(sc, second, first), by_parity(sc, first, second)


def edge_messages(row, ref, sends, places, width, margin, sc):
    count = ref.shape[0]
    row_messages(ref, sends[0], places[0], width, margin, sc)
    packed = []
    for code in (sc[2], sc[3]):
        first_lane = jnp.where(odd(code) == 1, width - margin, 0)
        packed.append(pack_columns(row, count, first_lane, code >= 2))
    near = [squeeze(part, PITCH * count) for part in packed]
    put_sides(sends[1:3], None, places[1], near[0], near[1], sc)
    far = [squeeze(shorten(part, count), 32) for part in packed]
    for index in range(sends[3].shape[0]):
        put_sides(sends[3:5], index, places[2], far[0], far[1], sc)


def pass_on(extras, sends, places):
    for extra, out, at, dim in zip(extras, sends, (places[0],) + (places[1],) * 2 + (places[2],) * 2, (1, 0, 0, 1, 1)):
        size = extra.shape[dim]
        if dim == 0:
            out[at : at + size] = extra[...]
        else:
            for index in range(extra.shape[0]):
                out[index, at : at + size] = extra[index]


def pair_rows(rows, margin):
    half = margin // 2
    lane = lane_of(rows[0].shape)
    return [jnp.where(lane < 64, rows[k], turn(rows[k + half], 64)) for k in range(half)]


def row_messages(ref, out, at, width, margin, sc):
    count, channels = ref.shape[0], ref.shape[1]
    for side in range(2):
        base = jnp.where(odd(sc[side]) == 1, count - margin, 0)
        picked = ref[pl.ds(base, margin)].reshape(margin * channels, LANES).astype(BF16)
        turned = matmul(picked, flipper(sc[side], width)).reshape(margin, channels, LANES)
        store_rows(turned, out, side, at, width, margin)


def store_rows(turned, out, side, at, width, margin):
    channels = turned.shape[1]
    slabs = channels // out.shape[-2]
    rows = [turned[k].astype(BF16) for k in range(margin)]
    if width == 64:
        rows = pair_rows(rows, margin)
    for k, slab in enumerate(rows):
        out[side, at + k * slabs : at + (k + 1) * slabs] = slab.reshape(
            (slabs, channels // slabs, LANES)
        )


def load_row(ref, side, at, k, channels, width, margin):
    slabs = channels // ref.shape[-2]
    half = margin // 2
    index = k % half if width == 64 else k
    slab = ref[side, at + index * slabs : at + (index + 1) * slabs].reshape(channels, LANES)
    return turn(slab, 64) if width == 64 and k >= half else slab


def rim_sides(first, second, base, width, margin, code):
    lane = lane_of(first.shape)
    rows = []
    for k in range(margin):
        left = turn(first, LANES - margin - PITCH * (base + k))
        right = turn(second, width - PITCH * (base + k))
        rows.append(jnp.where(lane >= LANES - margin, left, right))
    channels = first.shape[0]
    flat = jnp.concatenate(rows, axis=0)
    turned = matmul(flat, flipper(code, width)).astype(BF16).reshape(margin, channels, LANES)
    return [turned[k] for k in range(margin)]


def padded_sides(received, places, count, channels, width, margin, sc):
    left, right = get_sides(received[1:3], None, places[1], channels, PITCH * count, sc)
    lane = lane_of((channels, LANES))
    rims = []
    for index, code in ((0, sc[4]), (received[3].shape[0] - 1, sc[5])):
        rims.append(
            rim_sides(
                *get_sides(received[3:5], index, places[2], channels, 32, sc),
                short_base(code, count, margin),
                width,
                margin,
                code,
            )
        )
    center = []
    for r in range(count):
        center.append(
            jnp.where(
                lane >= LANES - margin,
                turn(left, LANES - margin - PITCH * r),
                turn(right, width - PITCH * r),
            )
        )
    return rims[0] + center + rims[1]


def padded_rows(tile, received, places, width, margin, sc):
    rows_in = received[0]
    count, channels = tile.shape[0], tile.shape[1]
    sides = padded_sides(received, places, count, channels, width, margin, sc)
    lane = lane_of((channels, LANES))
    for r in range(count + 2 * margin):
        if r < margin:
            own = load_row(rows_in, 1, places[0], r, channels, width, margin)
        elif r < margin + count:
            own = tile[r - margin]
        else:
            own = load_row(rows_in, 0, places[0], r - margin - count, channels, width, margin)
        if width == 64:
            own = jnp.where(lane < width, own, sides[r])
        yield r, own, sides[r]


def store_shifts(taps, r, at, step, own, sides, width, spacing):
    channels = own.shape[0]
    lane = lane_of(own.shape)
    if width == 64:
        from_left, from_right = own, own
    else:
        from_left = jnp.where(lane >= LANES - spacing, sides, own)
        from_right = jnp.where(lane < spacing, sides, own)
    taps[r, at : at + channels] = turn(from_left, spacing)
    taps[r, step + at : step + at + channels] = own
    taps[r, 2 * step + at : 2 * step + at + channels] = turn(from_right, -spacing)


def fill_taps(taps, tile, received, places, width, sc, spacing):
    channels = tile.shape[1]
    for r, own, sides in padded_rows(tile, received, places, width, DMAX, sc):
        store_shifts(taps, r, 0, channels, own, sides, width, spacing)


def tap_pair(taps, i, spacing):
    sections = []
    for row in (i, i + 1):
        sections.append(
            jnp.concatenate([taps[row + DMAX + (a - 1) * spacing] for a in range(3)], axis=0)
        )
    return jnp.concatenate(sections, axis=1)


def column_of(offset):
    return jnp.concatenate([offset[...], offset[...]], axis=1)


def normal_cdf(values):
    return 0.5 + 0.5 * lax.erf(values * (2.0**-0.5))


def gelu(values):
    return values * normal_cdf(values)


def gelu_slope(values):
    density = jnp.exp(-0.5 * values * values) * (1.0 / math.sqrt(2.0 * math.pi))
    return normal_cdf(values) + values * density


def pool_matrix(weight):
    row = lax.broadcasted_iota(jnp.int32, (2 * LANES, LANES), 0)
    col = lax.broadcasted_iota(jnp.int32, (2 * LANES, LANES), 1)
    return jnp.where(jnp.bitwise_and(row, LANES - 1) // 2 == col, weight, 0.0).astype(BF16)


def spread_matrix():
    row = lax.broadcasted_iota(jnp.int32, (LANES, LANES), 0)
    col = lax.broadcasted_iota(jnp.int32, (LANES, LANES), 1)
    return jnp.where(col // 2 == row, 1.0, 0.0).astype(BF16)


def side_spread_matrix():
    row = lax.broadcasted_iota(jnp.int32, (LANES, LANES), 0)
    col = lax.broadcasted_iota(jnp.int32, (LANES, LANES), 1)
    source = jnp.where(col >= 124, 126 + (col - 124) // 2, jnp.where(col < 4, 64 + col // 2, -1))
    return jnp.where(source == row, 1.0, 0.0).astype(BF16)


def fill_delta(delta, rows):
    count = delta.shape[0] - 16
    nothing = jnp.zeros((8,) + delta.shape[1:], BF16)
    delta[0:8] = nothing
    delta[8 + count :] = nothing
    for r in range(count):
        delta[8 + r] = rows(r)


def tap_products(delta, kernel, spacing, r):
    sections = []
    for row in (r, r + 1):
        sections.append(
            jnp.concatenate([delta[8 + row - DMAX - (a - 1) * spacing] for a in range(3)], axis=0)
        )
    return matmul(kernel[...], jnp.concatenate(sections, axis=1))


def move_taps(left, middle, right, spacing, width):
    lane = lane_of(middle.shape)
    to_left, to_right = turn(left, -spacing), turn(right, spacing)
    if width == 64:
        own = middle + to_left + to_right
        return own, own
    keep_right = lane >= spacing
    keep_left = lane < LANES - spacing
    own = middle + jnp.where(keep_right, to_right, 0.0) + jnp.where(keep_left, to_left, 0.0)
    sides = jnp.where(keep_right, 0.0, to_right) + jnp.where(keep_left, 0.0, to_left)
    return own, sides


def spread_taps(delta, kernel, spacing, width):
    count = delta.shape[0] - 16
    channels = kernel.shape[0] // 3
    for r in range(0, count + 2 * DMAX, 2):
        both = tap_products(delta, kernel, spacing, r)
        for k in range(2):
            part = both[:, k * LANES : (k + 1) * LANES]
            pieces = [part[e * channels : (e + 1) * channels] for e in range(3)]
            yield (r + k,) + move_taps(*pieces, spacing, width)


def rim_messages(own, sides, sends, places, width, margin, sc):
    rows_out = sends[0]
    total, channels = own.shape[0], own.shape[1]
    count = total - 2 * margin
    lane = lane_of((channels, LANES))
    near = []
    for first_lane in (-margin, width):
        packed = pack_columns(lambda r: sides[margin + r].astype(BF16), count, first_lane, None)
        near.append(squeeze(packed, PITCH * count))
    put_sides(sends[1:3], None, places[1], near[0], near[1], sc)
    corners = []
    for side, code, start in ((0, sc[4], 0), (1, sc[5], margin + count)):
        mirror = flipper(code, width)
        flat = own[start : start + margin].reshape(margin * channels, LANES).astype(BF16)
        turned = matmul(flat, mirror).reshape(margin, channels, LANES)
        store_rows(turned, rows_out, side, places[0], width, margin)
        if width != 64:
            flat = sides[start : start + margin].reshape(margin * channels, LANES).astype(BF16)
            turned = matmul(flat, mirror).reshape(margin, channels, LANES)
        base = short_base(code, count, margin)
        left = jnp.zeros((channels, LANES), F32)
        right = jnp.zeros((channels, LANES), F32)
        for k in range(margin):
            here = lane // PITCH == base + k
            left = jnp.where(here, turn(turned[k], PITCH * (base + k) + margin), left)
            right = jnp.where(here, turn(turned[k], PITCH * (base + k) - width), right)
        corners.append((squeeze(left, 32), squeeze(right, 32)))
    if sends[3].shape[0] == 1:
        both = [corners[0][i] + corners[1][i] for i in range(2)]
        put_sides(sends[3:5], 0, places[2], both[0], both[1], sc)
    else:
        for index in range(2):
            left, right = corners[1 - index]
            put_sides(sends[3:5], index, places[2], left, right, sc)


def fold(total, inner, received, places, width, margin, sc):
    rows_in = received[0]
    count, channels = inner.shape[0], inner.shape[1]
    lane = lane_of((channels, LANES))
    used = PITCH * count
    found = [
        side.astype(F32)
        for side in get_sides(received[1:3], None, places[1], channels, used, sc)
    ]
    for index in range(received[3].shape[0]):
        for i, short in enumerate(get_sides(received[3:5], index, places[2], channels, 32, sc)):
            short = short.astype(F32)
            if count <= 8:
                found[i] = found[i] + jnp.where(lane < 32, short, 0.0)
            else:
                late = turn(short, used - 32)
                late = jnp.where((lane >= used - 16) & (lane < used), late, 0.0)
                found[i] = found[i] + jnp.where(lane < 16, short, late)
    for r in range(count):
        row = inner[r]
        for packed, code in ((found[0], sc[2]), (found[1], sc[3])):
            first = jnp.where(odd(code) == 1, width - margin, 0)
            place = jnp.where(code >= 2, count - 1 - r, r)
            moved = turn(packed, first - PITCH * place)
            row = row + jnp.where((lane >= first) & (lane < first + margin), moved, 0.0)
        total[r] = row
    for side, code in ((0, sc[1]), (1, sc[0])):
        base = odd(code) * (count - margin)
        for k in range(margin):
            total[base + k] = total[base + k] + load_row(
                rows_in, side, places[0], k, channels, width, margin
            ).astype(F32)


START = (0, 0, 0)
AFTER_POOLED = (2, 1, 1)
AFTER_SECOND = (4, 2, 2)


def weights_kernel(jobs, swapped, *refs):
    layers = sorted({layer for _, layer in jobs})
    kernels = dict(zip(layers, refs))
    shifts = [layer for form, layer in jobs if form == 2]
    offsets = dict(zip(shifts, refs[len(layers) :]))
    outs = dict(zip(jobs, refs[len(layers) + len(shifts) :]))
    for layer in layers:
        kernel = kernels[layer]
        count, channels = kernel.shape[1:]
        if swapped[layer]:
            count, channels = channels, count
        for tap in range(9):
            a, e = tap // 3, tap % 3
            for form in range(2):
                if (form, layer) not in outs:
                    continue
                part = kernel[tap]
                if (form == 1) != swapped[layer]:
                    part = jnp.transpose(part.astype(F32)).astype(BF16)
                if form == 0:
                    outs[0, layer][:, tap * channels : (tap + 1) * channels] = part
                else:
                    rows = slice(e * channels, (e + 1) * channels)
                    outs[1, layer][rows, a * count : (a + 1) * count] = part
        if (2, layer) in outs:
            row = lax.broadcasted_iota(jnp.int32, (count, count), 0)
            col = lax.broadcasted_iota(jnp.int32, (count, count), 1)
            column = jnp.where(row == col, offsets[layer][...], 0.0)
            column = jnp.sum(column, axis=1, keepdims=True)
            outs[2, layer][...] = jnp.broadcast_to(column, outs[2, layer].shape)


def fields_kernel(sc, fields, tile, *sends):
    tile[...] = jnp.swapaxes(fields[...], 0, 1)
    edge_messages(lambda r: tile[r], tile, sends, START, LANES, DMAX, sc)
    last, shape = sends[0].shape[1] - 1, sends[0].shape[2:]
    for side in range(2):
        code = sc[side].astype(F32)
        sends[0][side, last] = jnp.broadcast_to(code, shape).astype(BF16)


def first_kernel(own_sc, tile, *refs):
    received, (kernel, offset) = refs[:5], refs[5:7]
    act_out, pre_out, pooled_out, sc, taps = refs[7:12]
    sends = refs[12:]
    last = received[0].shape[1] - 1
    for i in range(13):
        sc[i] = own_sc[i]
    for i in range(2):
        sc[4 + i] = jnp.max(received[0][1 - i, last].astype(F32)).astype(jnp.int32)
    spacing = own_sc[6]
    fill_taps(taps, tile, received, START, LANES, sc, spacing)
    pool = pool_matrix(0.25)
    shift = column_of(offset)
    for i in range(0, tile.shape[0], 2):
        pre = matmul(kernel[...], tap_pair(taps, i, spacing)) + shift
        act = gelu(pre).astype(BF16)
        for k in range(2):
            act_out[i + k] = act[:, k * LANES : (k + 1) * LANES]
            pre_out[i + k] = pre[:, k * LANES : (k + 1) * LANES]
        pooled_out[i // 2] = matmul(act, pool).astype(BF16)
    edge_messages(
        lambda r: pooled_out[r], pooled_out, sends, START, 64, DMAX, sc
    )
    edge_messages(
        lambda r: act_out[r], act_out, sends, AFTER_POOLED, LANES, DMAX, sc
    )


def second_kernel(sc, tile, *refs):
    received, (kernel, offset), extras = refs[:5], refs[5:7], refs[7:12]
    act_out, pre_out, taps = refs[12:15]
    sends = refs[15:]
    spacing = sc[7]
    fill_taps(taps, tile, received, START, 64, sc, spacing)
    shift = column_of(offset)
    for i in range(0, tile.shape[0], 2):
        pre = matmul(kernel[...], tap_pair(taps, i, spacing)) + shift
        act = gelu(pre).astype(BF16)
        for k in range(2):
            act_out[i + k] = act[:, k * LANES : (k + 1) * LANES]
            pre_out[i + k] = pre[:, k * LANES : (k + 1) * LANES]
    edge_messages(lambda r: act_out[r], act_out, sends, START, 64, DMAX, sc)
    pass_on(extras, sends, AFTER_SECOND)


def slopes_kernel(*refs):
    half = len(refs) // 2
    for values, out in zip(refs[:half], refs[half:]):
        for r in range(values.shape[0]):
            out[r] = gelu_slope(values[r])


def masked(values, width):
    return jnp.where(lane_of(values.shape) < width, values, 0.0).astype(BF16)


def back_part(sc, delta, kernel, spacing, width, inner_out, sends, own_all, sides_all):
    count = delta.shape[0] - 16
    for r, own, sides in spread_taps(delta, kernel, spacing, width):
        own_all[r] = own
        if width != 64:
            sides_all[r] = sides
    for r in range(count):
        inner_out[r] = own_all[DMAX + r]
    rim_messages(own_all, sides_all, sends, START, width, DMAX, sc)


def third_kernel(sc, tile, *refs):
    received, (kernel, offset, coarse, back) = refs[:5], refs[5:9]
    act_out, delta_out, inner_out = refs[9:12]
    sends, (taps, delta, own_all, coarse_sum) = refs[12:17], refs[17:]
    fold(coarse_sum, coarse, received, AFTER_SECOND, 64, 2, sc)
    spacing = sc[8]
    fill_taps(taps, tile, received, START, 64, sc, spacing)
    shift = column_of(offset)
    for i in range(0, tile.shape[0], 2):
        pre = matmul(kernel[...], tap_pair(taps, i, spacing)) + shift
        act, slope = gelu(pre), gelu_slope(pre)
        for k in range(2):
            act_out[i + k] = act[:, k * LANES : (k + 1) * LANES].astype(BF16)
            delta_out[i + k] = masked(
                coarse_sum[i + k] * slope[:, k * LANES : (k + 1) * LANES], 64
            )
    fill_delta(delta, lambda r: delta_out[r])
    back_part(sc, delta, back, spacing, 64, inner_out, sends, own_all, own_all)
    edge_messages(lambda r: act_out[r], act_out, sends, AFTER_SECOND, 64, 2, sc)


def middle_kernel(sc, inner, *refs):
    received, (slope, back), extras = refs[:5], refs[5:7], refs[7:12]
    delta_out, inner_out = refs[12:14]
    sends, (total, delta, own_all) = refs[14:19], refs[19:]
    fold(total, inner, received, START, 64, DMAX, sc)
    for r in range(inner.shape[0]):
        delta_out[r] = masked(total[r] * slope[r], 64)
    fill_delta(delta, lambda r: delta_out[r])
    back_part(sc, delta, back, sc[7], 64, inner_out, sends, own_all, own_all)
    pass_on(extras, sends, AFTER_POOLED)


def lower_kernel(sc, inner, *refs):
    received, (slope, skip_inner, back) = refs[:5], refs[5:8]
    delta_out, inner_out = refs[8:10]
    sends, (total, skip, delta, own_all, sides_all) = refs[10:15], refs[15:]
    fold(total, inner, received, START, 64, DMAX, sc)
    fold(skip, skip_inner, received, AFTER_POOLED, LANES, DMAX, sc)
    spread = spread_matrix()
    for r in range(inner.shape[0]):
        lane = lane_of(total[r].shape)
        high, low = halves(jnp.where(lane < 64, total[r], 0.0))
        wide = 0.25 * (matmul(high, spread) + matmul(low, spread))
        for k in range(2):
            row = 2 * r + k
            delta_out[row] = ((skip[row] + wide) * slope[row]).astype(BF16)
    fill_delta(delta, lambda r: delta_out[r])
    back_part(sc, delta, back, sc[6], LANES, inner_out, sends, own_all, sides_all)


def last_kernel(sc, inner, *refs):
    received, out, total = refs[:5], refs[5], refs[6]
    fold(total, inner, received, START, LANES, DMAX, sc)
    out[...] = jnp.swapaxes(total[...], 0, 1)


def moved_pool_matrix(spacing):
    row = lax.broadcasted_iota(jnp.int32, (2 * LANES, LANES), 0)
    col = lax.broadcasted_iota(jnp.int32, (2 * LANES, LANES), 1)
    parts = []
    for e in range(3):
        target = jnp.right_shift(jnp.bitwise_and(row, LANES - 1) + (e - 1) * spacing, 1)
        hit = jnp.bitwise_and(target, LANES - 1) == col
        parts.append(jnp.where(hit, 1.0, 0.0).astype(BF16))
    return jnp.concatenate(parts, axis=0)


def upstream_kernel(sc, cotangent, closing, *refs):
    upstream, coarse_out, skip_out = refs[:3]
    coarse_sends, skip_sends = refs[3:8], refs[8:13]
    delta, own_all, sides_all, coarse_all, back, high_all, low_all = refs[13:]
    outs, channels = closing.shape[1:]
    for tap in range(9):
        a, e = tap // 3, tap % 3
        across = jnp.transpose(closing[tap].astype(F32)).astype(BF16)
        back[e * channels : (e + 1) * channels, a * outs : (a + 1) * outs] = across
    upstream[...] = jnp.swapaxes(cotangent[...], 0, 1)
    fill_delta(delta, lambda r: upstream[r])
    spacing = sc[9]
    pool = moved_pool_matrix(spacing)
    skips = own_all.shape[1]
    coarse = channels - skips
    for r in range(0, own_all.shape[0], 2):
        both = tap_products(delta, back, spacing, r)
        parts = [both[e * channels : (e + 1) * channels] for e in range(3)]
        high, low = halves(jnp.concatenate([part[:coarse] for part in parts], axis=1))
        at = r // 2 * coarse
        high_all[at : at + coarse] = high
        low_all[at : at + coarse] = low
        for k in range(2):
            lanes = slice(k * LANES, (k + 1) * LANES)
            own, sides = move_taps(*[part[coarse:, lanes] for part in parts], spacing, LANES)
            own_all[r + k] = own
            sides_all[r + k] = sides
    pooled = matmul(high_all[...], pool) + matmul(low_all[...], pool)
    coarse_all[...] = pooled.reshape(coarse_all.shape)
    for r in range(coarse_out.shape[0]):
        coarse_out[r] = coarse_all[2 + r]
    for r in range(skip_out.shape[0]):
        skip_out[r] = own_all[4 + r]
    rim_messages(coarse_all, coarse_all, coarse_sends, START, 64, 2, sc)
    rim_messages(own_all, sides_all, skip_sends, START, LANES, 4, sc)


def put_terms(out, at, sums, sides):
    outs, columns = sums.shape
    whole = columns // LANES
    for k in range(whole):
        out[at + k * outs : at + (k + 1) * outs] = sums[:, k * LANES : (k + 1) * LANES].astype(BF16)
    if columns % LANES:
        wide = jnp.concatenate(
            [jnp.broadcast_to(side, (outs, 64 // len(sides))) for side in sides], axis=1
        )
        tail = jnp.concatenate([sums[:, whole * LANES :], wide], axis=1)
        out[at + whole * outs : at + (whole + 1) * outs] = tail.astype(BF16)


def row_sum(rows):
    total = None
    for r in range(rows.shape[0]):
        row = rows[r].astype(F32)
        total = row if total is None else total + row
    return jnp.sum(total, axis=1, keepdims=True)


def layer_terms(taps, delta, spacing, use=None):
    sums = None
    for i in range(0, delta.shape[0], 2):
        section = tap_pair(taps, i, spacing)
        if use is not None:
            use(i, section)
        part = matmul_t(jnp.concatenate([delta[i], delta[i + 1]], axis=1), section)
        sums = part if sums is None else sums + part
    return sums


def third_terms_kernel(sc, second, delta, *refs):
    third_in, (out, taps) = refs[:5], refs[5:]
    fill_taps(taps, second, third_in, START, 64, sc, sc[8])
    put_terms(out, 0, layer_terms(taps, delta, sc[8]), None)


def joined_kernel(
    sc, coarse, fine, taps_second, delta_third, delta_second, upstream, kernel, offset, *refs
):
    second_in, back_in = refs[:5], refs[5:10]
    state_out, out, taps, state_all = refs[10:]
    sums = layer_terms(taps_second, delta_second, sc[7])
    put_terms(out, 0, sums, [row_sum(delta_second), row_sum(delta_third)])
    after = -(-sums.shape[1] // LANES) * sums.shape[0]
    spacing = sc[9]
    spread = jnp.concatenate([spread_matrix(), side_spread_matrix()], axis=1)
    for r, own, _ in padded_rows(coarse, back_in, AFTER_SECOND, 64, 2, sc):
        wide = matmul(own, spread).astype(BF16)
        for k in range(2):
            store_shifts(
                taps, 2 * r + k, 0, 192, wide[:, :LANES], wide[:, LANES:], LANES, spacing
            )
    for r, own, sides in padded_rows(fine, second_in, AFTER_POOLED, LANES, 4, sc):
        store_shifts(taps, r, 128, 192, own, sides, LANES, spacing)
    shift = column_of(offset)

    def use(i, section):
        state = (matmul(kernel[...], section) + shift).astype(BF16)
        for k in range(2):
            state_all[i + k] = state[:, k * LANES : (k + 1) * LANES]

    put_terms(out, after, layer_terms(taps, upstream, spacing, use), [row_sum(upstream)])
    state_out[...] = jnp.swapaxes(state_all[...], 0, 1)


def first_terms_kernel(sc, taps, delta, third_terms, terms, give, keep, whole):
    rows = 0
    for part in (third_terms, terms):
        whole[rows : rows + part.shape[0]] = part[...]
        rows += part.shape[0]
    sums = layer_terms(taps, delta, sc[6])
    put_terms(whole, rows, sums, [row_sum(delta)])
    rows += -(-sums.shape[1] // LANES) * sums.shape[0]
    whole[rows:] = jnp.zeros((whole.shape[0] - rows, LANES), BF16)
    half = keep.shape[0]
    keep[...] = whole[pl.ds(pl.multiple_of(sc[10] * half, 16), half)]
    give[...] = whole[pl.ds(pl.multiple_of((1 - sc[10]) * half, 16), half)]


def core_sum_kernel(sc, keep, given, own, *gives):
    size = own.shape[0]
    for i, out in enumerate((own,) + gives):
        member = sc[11] if i < 2 else 1 - sc[11]
        chip = sc[12] if i % 2 == 0 else 1 - sc[12]
        rows = pl.ds(pl.multiple_of((2 * member + chip) * size, 16), size)
        out[...] = (keep[rows].astype(F32) + given[rows].astype(F32)).astype(out.dtype)


def adding_kernel(*refs):
    total = refs[0][...].astype(F32)
    for ref in refs[1:-1]:
        total = total + ref[...].astype(F32)
    refs[-1][...] = total.astype(BF16)


def unpack_kernel(scale, layouts, biases, sc, *refs):
    eighths, outs, summed = refs[:8], refs[8:-1], refs[-1]
    size = eighths[0].shape[0]
    for i, eighth in enumerate(eighths):
        bits = [sc[10 + k] if (i >> (2 - k)) % 2 == 0 else 1 - sc[10 + k] for k in range(3)]
        at = pl.multiple_of((4 * bits[0] + 2 * bits[1] + bits[2]) * size, 16)
        summed[pl.ds(at, size)] = eighth[...]
    for (start, outs_count, channels, swapped), out in zip(layouts, outs):
        def slab_at(slab):
            first = start + slab * outs_count
            return summed[first : first + outs_count].astype(F32) * scale

        if swapped:
            for slab in range(5):
                across = jnp.transpose(slab_at(slab))
                for tap in range(2 * slab, min(2 * slab + 2, 9)):
                    at = (tap - 2 * slab) * channels
                    out[tap] = across[at : at + channels]
            continue
        for tap in range(9):
            first, last = tap * channels, (tap + 1) * channels
            found = []
            while first < last:
                slab = first // LANES
                end = min(last, (slab + 1) * LANES)
                found.append(slab_at(slab)[:, first - slab * LANES : end - slab * LANES])
                first = end
            out[tap] = found[0] if len(found) == 1 else jnp.concatenate(found, axis=1)
    for (start, count, lane), out in zip(biases, outs[len(layouts) :]):
        block = summed[start : start + count].astype(F32)
        column = jnp.sum(
            jnp.where(lane_of(block.shape) == lane, block, 0.0), axis=1, keepdims=True
        )
        row = lax.broadcasted_iota(jnp.int32, (count, count), 0)
        col = lax.broadcasted_iota(jnp.int32, (count, count), 1)
        out[...] = jnp.sum(jnp.where(row == col, column, 0.0), axis=0, keepdims=True) * scale


def call(body, inputs, outputs, scratch=(), flops=0, scalars=1, name=None):
    specs = [pl.BlockSpec(memory_space=pltpu.VMEM)] * len(inputs)
    for i in range(scalars):
        specs[i] = pl.BlockSpec(memory_space=pltpu.SMEM)
    moved = sum(math.prod(shape) * jnp.dtype(kind).itemsize for shape, kind in outputs)
    moved += sum(array.size * array.dtype.itemsize for array in inputs)
    spaces = [pltpu.SMEM if kind == jnp.int32 else pltpu.VMEM for _, kind in outputs]
    return pl.pallas_call(
        body,
        out_shape=[jax.ShapeDtypeStruct(shape, kind) for shape, kind in outputs],
        in_specs=specs,
        out_specs=[pl.BlockSpec(memory_space=space) for space in spaces],
        scratch_shapes=[pltpu.VMEM(shape, kind) for shape, kind in scratch],
        compiler_params=pltpu.CompilerParams(vmem_limit_bytes=24 * 1024 * 1024),
        cost_estimate=pl.CostEstimate(flops=flops, bytes_accessed=moved, transcendentals=0),
        name=name,
    )(*inputs)


def shifted(array, for_even, for_odd):
    devices = lax.axis_size("tile")
    pairs = [(i, (i + (for_odd if i % 2 else for_even)) % devices) for i in range(devices)]
    return lax.ppermute(array, "tile", pairs)


def wrapped():
    return lax.axis_size("tile") == 2 * TILE_ROW


def other_tile(array, bit):
    pairs = [(i, i ^ (1 << bit)) for i in range(lax.axis_size("tile"))]
    return lax.ppermute(array, "tile", pairs)


def other_member(array):
    return lax.ppermute(array, "ens", [(0, 1), (1, 0)])


def other_both(array, bit):
    tiles = lax.axis_size("tile")
    pairs = [(i, (i ^ (1 << bit)) + tiles if i < tiles else (i ^ (1 << bit)) - tiles)
             for i in range(2 * tiles)]
    return lax.ppermute(array, ("ens", "tile"), pairs)


def exchange_rows(rows):
    if wrapped():
        return shifted(rows, TILE_ROW, TILE_ROW)
    return jnp.stack(
        [shifted(rows[0], -TILE_ROW, -TILE_ROW), shifted(rows[1], TILE_ROW, TILE_ROW)]
    )


def exchange(rows, near_a, near_b, far_a, far_b):
    row = TILE_ROW
    rows_in = exchange_rows(rows)
    if wrapped():
        a_in = shifted(far_a, row + 1, row - 1)
        b_in = shifted(far_b, row - 1, row + 1)
    else:
        a_in = jnp.stack(
            [shifted(far_a[0], row + 1, row - 1), shifted(far_a[1], 1 - row, -1 - row)]
        )
        b_in = jnp.stack(
            [shifted(far_b[0], row - 1, row + 1), shifted(far_b[1], -1 - row, 1 - row)]
        )
    return [rows_in, shifted(near_a, 1, -1), shifted(near_b, -1, 1), a_in, b_in]


def shards(
    fields,
    cotangent,
    kernel_first,
    kernel_second,
    kernel_third,
    closing_filter_weights,
    offset_first,
    offset_second,
    offset_third,
    closing_shift_values,
    codes,
    filter_stride_spread,
):
    members, _, low, height, width = fields.shape
    high = kernel_third.shape[1]
    half = height // 2
    fars = 1 if wrapped() else 2
    tile_index = lax.axis_index("tile")
    place = [tile_index & 1, lax.axis_index("ens") & 1, (tile_index >> 1) & 1]
    own_sc = jnp.concatenate(
        [codes[0], jnp.zeros((2,), jnp.int32), filter_stride_spread]
        + [bit.astype(jnp.int32)[None] for bit in place]
    )

    def sends(rows, near, far):
        return (
            [((2, rows, 64, LANES), BF16)]
            + [((near, 16, LANES), BF16)] * 2
            + [((fars, far, 16, LANES), BF16)] * 2
        )

    fine_tile = ((height, low, LANES), BF16)
    fine_grad = ((height, low, LANES), F32)
    tile, *sent = call(
        fields_kernel,
        [own_sc, fields[0, 0]],
        [fine_tile, ((2, DMAX * low // 16 + 1, 16, LANES), BF16)] + sends(5, 2, 1)[1:],
        name="fields_edges",
    )
    first_in = exchange(*sent)

    weights = [kernel_first, kernel_second, kernel_third, closing_filter_weights]
    offsets = [offset_first, offset_second, offset_third, closing_shift_values]
    swapped = [k.shape[1] % LANES == 0 and k.shape[2] % LANES != 0 for k in weights]
    def prepare(jobs, kernels, name):
        layers = sorted({layer for _, layer in jobs})
        inputs = [jnp.swapaxes(kernels[i], 1, 2) if swapped[i] else kernels[i] for i in layers]
        outputs = []
        for form, layer in jobs:
            _, count, channels = kernels[layer].shape
            shapes = [(count, 9 * channels), (3 * channels, 3 * count), (count, LANES)]
            outputs.append((shapes[form], F32 if form == 2 else BF16))
        made = call(
            functools.partial(weights_kernel, jobs, swapped),
            inputs + [offsets[layer][None] for form, layer in jobs if form == 2],
            outputs,
            scalars=0,
            name=name,
        )
        return dict(zip(jobs, made))

    forms = prepare([(0, 0), (0, 1), (2, 0), (2, 1)], weights, "early_weights")

    first_taps = ((height + 8, 3 * low, LANES), BF16)
    act_first, pre_first, pooled, sc, taps_first, *sent = call(
        first_kernel,
        [own_sc, tile, *first_in, forms[0, 0], forms[2, 0]],
        [fine_tile, fine_grad, ((half, low, LANES), BF16), ((13,), jnp.int32), first_taps]
        + sends(6, 3, 2),
        flops=2 * 9 * low * low * height * width,
        name="first_layer",
    )
    second_in = exchange(*sent)

    upstream, coarse_inner, skip_inner, *rims = call(
        upstream_kernel,
        [sc, cotangent[0, 0], closing_filter_weights],
        [fine_tile, ((half, high, LANES), F32), fine_grad] + sends(2, 2, 2) + sends(4, 2, 1),
        [
            ((height + 16, low, LANES), BF16),
            ((height + 8, low, LANES), F32),
            ((height + 8, low, LANES), F32),
            ((half + 4, high, LANES), F32),
            ((3 * (low + high), 3 * low), BF16),
            (((half + 4) * high, 6 * LANES), BF16),
            (((half + 4) * high, 6 * LANES), BF16),
        ],
        flops=2 * 9 * low * (low + high) * height * width,
        name="cotangent_back",
    )
    coarse_rims, skip_rims = rims[:5], rims[5:]

    second_taps = ((half + 8, 3 * low, LANES), BF16)
    act_second, pre_second, taps_second, *sent = call(
        second_kernel,
        [sc, pooled, *second_in, forms[0, 1], forms[2, 1], *coarse_rims],
        [((half, high, LANES), BF16), ((half, high, LANES), F32), second_taps]
        + sends(6, 4, 4),
        flops=2 * 9 * low * high * half * LANES,
        name="second_layer",
    )
    third_in = exchange(*sent)
    late_third, pre_second = lax.optimization_barrier((kernel_third, pre_second))
    forms.update(
        prepare(
            [(0, 2), (0, 3), (1, 0), (1, 1), (1, 2), (2, 2), (2, 3)],
            weights[:2] + [late_third] + weights[3:],
            "late_weights",
        )
    )
    slope_first, slope_second = call(
        slopes_kernel,
        [pre_first, pre_second],
        [fine_grad, ((half, high, LANES), F32)],
        scalars=0,
        name="slopes",
    )
    coarse_inner, slope_first = lax.optimization_barrier((coarse_inner, slope_first))

    third_taps = ((half + 8, 3 * high, LANES), BF16)
    act_third, delta_third, inner, *sent = call(
        third_kernel,
        [sc, act_second, *third_in, forms[0, 2], forms[2, 2], coarse_inner, forms[1, 2]],
        [((half, high, LANES), BF16)] * 2 + [((half, high, LANES), F32)] + sends(6, 4, 4),
        [
            third_taps,
            ((half + 16, high, LANES), BF16),
            ((half + 8, high, LANES), F32),
            ((half, high, LANES), F32),
        ],
        flops=2 * 2 * 9 * high * high * half * LANES,
        name="third_layer_and_back",
    )
    back_in = exchange(*sent)
    (third_terms,) = call(
        third_terms_kernel,
        [sc, act_second, delta_third, *third_in],
        [((9 * high, LANES), BF16)],
        [third_taps],
        flops=2 * 9 * high * high * half * LANES,
        name="third_terms",
    )
    inner, third_terms = lax.optimization_barrier((inner, third_terms))

    delta_second, inner, *sent = call(
        middle_kernel,
        [sc, inner, *back_in, slope_second, forms[1, 1], *skip_rims],
        [((half, high, LANES), BF16), ((half, low, LANES), F32)] + sends(6, 3, 2),
        [
            ((half, high, LANES), F32),
            ((half + 16, high, LANES), BF16),
            ((half + 8, low, LANES), F32),
        ],
        flops=2 * 9 * low * high * half * LANES,
        name="second_back",
    )
    lower_in = exchange(*sent)

    narrow = -(-9 * low // LANES)
    wide = -(-9 * (low + high) // LANES)
    upper_rows = narrow * high + wide * low
    state, upper_terms = call(
        joined_kernel,
        [
            sc, act_third, act_first, taps_second, delta_third, delta_second, upstream, forms[0, 3],
            forms[2, 3], *second_in, *back_in,
        ],
        [((low, height, LANES), BF16), ((upper_rows, LANES), BF16)],
        [
            ((height + 8, 3 * (low + high), LANES), BF16),
            fine_tile,
        ],
        flops=2 * 2 * 9 * low * (low + high) * height * width,
        name="joined_layer_and_terms",
    )
    lower_in[0], upper_terms = lax.optimization_barrier((lower_in[0], upper_terms))

    delta_first, inner, *sent = call(
        lower_kernel,
        [sc, inner, *lower_in, slope_first, skip_inner, forms[1, 0]],
        [fine_tile, fine_grad] + sends(4, 2, 1),
        [
            ((half, low, LANES), F32),
            fine_grad,
            ((height + 16, low, LANES), BF16),
            ((height + 8, low, LANES), F32),
            ((height + 8, low, LANES), F32),
        ],
        flops=2 * 9 * low * low * height * width,
        name="first_back",
    )

    tiles = lax.axis_size("tile")
    rows = 9 * high + upper_rows + narrow * low
    size = -(-rows // (8 * 16)) * 16

    def part(count):
        return ((count * size, LANES), BF16)

    give, keep = call(
        first_terms_kernel,
        [sc, taps_first, delta_first, third_terms, upper_terms],
        [part(4)] * 2,
        [part(8)],
        flops=2 * 9 * low * low * height * width,
        name="first_terms",
    )
    given = other_tile(give, 0)
    own, *gives = call(
        core_sum_kernel,
        [sc, keep, given],
        [((size, LANES), F32)] + [part(1)] * 3,
        name="core_sum",
    )
    given = [other_tile(gives[0], 1), other_member(gives[1]), other_both(gives[2], 1)]
    last_in = exchange(*sent)
    own, last_in[0] = lax.optimization_barrier((own, last_in[0]))
    (total,) = call(adding_kernel, [own, *given], [part(1)], scalars=0, name="chip_sum")
    last_bit = tiles.bit_length() - 2
    for bit in range(2, last_bit + 1):
        if bit == last_bit:
            total, last_in[1], last_in[2] = lax.optimization_barrier(
                (total, last_in[1], last_in[2])
            )
        given = other_tile(total, bit)
        (total,) = call(adding_kernel, [total, given], [part(1)], scalars=0, name=f"sum_{bit}")
    (derivative,) = call(
        last_kernel,
        [sc, inner, *last_in],
        [((low, height, LANES), F32)],
        [fine_grad],
        name="last_fold",
    )

    total, derivative = lax.optimization_barrier((total, derivative))
    eighths = [total, other_tile(total, 1), other_member(total), other_both(total, 1)]
    eighths = eighths + [other_tile(eighth, 0) for eighth in eighths]

    all_tiles = members * lax.axis_size("ens") * lax.axis_size("tile")
    scale = 1.0 / math.sqrt(all_tiles * height * width)
    upper_rows += 9 * high
    starts = [upper_rows, 9 * high, 0, upper_rows - wide * low]
    layouts = [
        (start, k.shape[1], k.shape[2], swap) for start, k, swap in zip(starts, weights, swapped)
    ]
    tail = 9 * high + (narrow - 1) * high
    biases = [(rows - low, low, 64), (tail, high, 64), (tail, high, 96), (upper_rows - low, low, 64)]
    grads = call(
        functools.partial(unpack_kernel, scale, layouts, biases),
        [sc, *eighths],
        [
            ((9, channels, outs) if swap else (9, outs, channels), F32)
            for _, outs, channels, swap in layouts
        ]
        + [((1, count), F32) for _, count, _ in biases],
        [part(8)],
        name="unpack_sums",
    )
    return (
        state[None, None],
        derivative[None, None],
        *[jnp.swapaxes(g, 1, 2) if swap else g for g, swap in zip(grads[:4], swapped)],
        *[grad[0] for grad in grads[4:]],
    )


def solution(mesh):
    tiles = P("ens", "tile", None, None, None)
    in_specs = (tiles, tiles) + (P(),) * 8 + (P("tile", None), P())
    out_specs = (tiles, tiles) + (P(),) * 8
    return jax.shard_map(shards, mesh=mesh, in_specs=in_specs, out_specs=out_specs, check_vma=False)
```

```python
import functools
import math

import jax
import jax.numpy as jnp
from jax import lax
from jax.experimental import pallas as pl
from jax.experimental.pallas import tpu as pltpu
from jax.sharding import PartitionSpec as P

DMAX = 4
TILE_ROW = 8
LANES = 128
PITCH = 4
F32 = jnp.float32
BF16 = jnp.bfloat16


def lane_of(shape):
    return lax.broadcasted_iota(jnp.int32, shape, len(shape) - 1)


def turn(slab, by):
    if isinstance(by, int):
        by = by % LANES
        if by == 0:
            return slab
    else:
        by = jnp.bitwise_and(by, LANES - 1)
    return pltpu.roll(slab, by, axis=slab.ndim - 1)


def odd(code):
    return jnp.bitwise_and(code, 1)


def flipper(code, width):
    first = lax.broadcasted_iota(jnp.int32, (LANES, LANES), 0)
    second = lax.broadcasted_iota(jnp.int32, (LANES, LANES), 1)
    mirrored = jnp.bitwise_and(width - 1 - first, LANES - 1)
    target = jnp.where(code >= 2, mirrored, first)
    return jnp.where(second == target, 1.0, 0.0).astype(BF16)


def matmul(left, right):
    return jnp.dot(left, right, preferred_element_type=F32)


def matmul_t(left, right):
    return lax.dot_general(left, right, (((1,), (1,)), ((), ())), preferred_element_type=F32)


def halves(values):
    high = values.astype(BF16)
    return high, (values - high.astype(F32)).astype(BF16)


def pack_columns(row, count, first_lane, flip):
    packed = None
    for r in range(count):
        place = r if flip is None else jnp.where(flip, count - 1 - r, r)
        moved = turn(row(r), PITCH * place - first_lane)
        if packed is None:
            packed = moved
        else:
            packed = jnp.where(lane_of(moved.shape) // PITCH == place, moved, packed)
    return packed


def squeeze(packed, used):
    groups = LANES // used
    part = packed.shape[0] // groups
    lane = lane_of((part, LANES))
    whole = packed[:part]
    for g in range(1, groups):
        moved = turn(packed[g * part : (g + 1) * part], used * g)
        whole = jnp.where(lane // used == g, moved, whole)
    return whole


def expand(whole, used):
    groups = LANES // used
    return jnp.concatenate([turn(whole, -used * g) for g in range(groups)], axis=0)


def shorten(packed, count):
    if count <= 8:
        return packed
    return jnp.where(lane_of(packed.shape) < 16, packed, turn(packed, 32 - PITCH * count))


def short_base(code, count, margin):
    return odd(code) * (min(count, 8) - margin)


def units_of(channels, used):
    return channels * used // (LANES * 16)


def put_units(ref, index, at, whole):
    units = whole.shape[0] // 16
    shaped = whole.reshape(units, 16, LANES).astype(BF16)
    if index is None:
        ref[at : at + units] = shaped
    else:
        ref[index, at : at + units] = shaped


def get_units(ref, index, at, channels, used):
    units = units_of(channels, used)
    block = ref[at : at + units] if index is None else ref[index, at : at + units]
    return expand(block.reshape(units * 16, LANES), used)


def by_parity(sc, for_even, for_odd):
    return jnp.where(sc[10] == 0, for_even, for_odd)


def put_sides(refs, index, at, leftward, rightward, sc):
    put_units(refs[0], index, at, by_parity(sc, rightward, leftward))
    put_units(refs[1], index, at, by_parity(sc, leftward, rightward))


def get_sides(refs, index, at, channels, used, sc):
    first = get_units(refs[0], index, at, channels, used)
    second = get_units(refs[1], index, at, channels, used)
    return by_parity(sc, second, first), by_parity(sc, first, second)


def edge_messages(row, ref, sends, places, width, margin, sc):
    count = ref.shape[0]
    row_messages(ref, sends[0], places[0], width, margin, sc)
    packed = []
    for code in (sc[2], sc[3]):
        first_lane = jnp.where(odd(code) == 1, width - margin, 0)
        packed.append(pack_columns(row, count, first_lane, code >= 2))
    near = [squeeze(part, PITCH * count) for part in packed]
    put_sides(sends[1:3], None, places[1], near[0], near[1], sc)
    far = [squeeze(shorten(part, count), 32) for part in packed]
    for index in range(sends[3].shape[0]):
        put_sides(sends[3:5], index, places[2], far[0], far[1], sc)


def pass_on(extras, sends, places):
    for extra, out, at, dim in zip(extras, sends, (places[0],) + (places[1],) * 2 + (places[2],) * 2, (1, 0, 0, 1, 1)):
        size = extra.shape[dim]
        if dim == 0:
            out[at : at + size] = extra[...]
        else:
            for index in range(extra.shape[0]):
                out[index, at : at + size] = extra[index]


def pair_rows(rows, margin):
    half = margin // 2
    lane = lane_of(rows[0].shape)
    return [jnp.where(lane < 64, rows[k], turn(rows[k + half], 64)) for k in range(half)]


def row_messages(ref, out, at, width, margin, sc):
    count, channels = ref.shape[0], ref.shape[1]
    for side in range(2):
        base = jnp.where(odd(sc[side]) == 1, count - margin, 0)
        picked = ref[pl.ds(base, margin)].reshape(margin * channels, LANES).astype(BF16)
        turned = matmul(picked, flipper(sc[side], width)).reshape(margin, channels, LANES)
        store_rows(turned, out, side, at, width, margin)


def store_rows(turned, out, side, at, width, margin):
    channels = turned.shape[1]
    slabs = channels // out.shape[-2]
    rows = [turned[k].astype(BF16) for k in range(margin)]
    if width == 64:
        rows = pair_rows(rows, margin)
    for k, slab in enumerate(rows):
        out[side, at + k * slabs : at + (k + 1) * slabs] = slab.reshape(
            (slabs, channels // slabs, LANES)
        )


def load_row(ref, side, at, k, channels, width, margin):
    slabs = channels // ref.shape[-2]
    half = margin // 2
    index = k % half if width == 64 else k
    slab = ref[side, at + index * slabs : at + (index + 1) * slabs].reshape(channels, LANES)
    return turn(slab, 64) if width == 64 and k >= half else slab


def rim_sides(first, second, base, width, margin, code):
    lane = lane_of(first.shape)
    rows = []
    for k in range(margin):
        left = turn(first, LANES - margin - PITCH * (base + k))
        right = turn(second, width - PITCH * (base + k))
        rows.append(jnp.where(lane >= LANES - margin, left, right))
    channels = first.shape[0]
    flat = jnp.concatenate(rows, axis=0)
    turned = matmul(flat, flipper(code, width)).astype(BF16).reshape(margin, channels, LANES)
    return [turned[k] for k in range(margin)]


def padded_sides(received, places, count, channels, width, margin, sc):
    left, right = get_sides(received[1:3], None, places[1], channels, PITCH * count, sc)
    lane = lane_of((channels, LANES))
    rims = []
    for index, code in ((0, sc[4]), (received[3].shape[0] - 1, sc[5])):
        rims.append(
            rim_sides(
                *get_sides(received[3:5], index, places[2], channels, 32, sc),
                short_base(code, count, margin),
                width,
                margin,
                code,
            )
        )
    center = []
    for r in range(count):
        center.append(
            jnp.where(
                lane >= LANES - margin,
                turn(left, LANES - margin - PITCH * r),
                turn(right, width - PITCH * r),
            )
        )
    return rims[0] + center + rims[1]


def padded_rows(tile, received, places, width, margin, sc):
    rows_in = received[0]
    count, channels = tile.shape[0], tile.shape[1]
    sides = padded_sides(received, places, count, channels, width, margin, sc)
    lane = lane_of((channels, LANES))
    for r in range(count + 2 * margin):
        if r < margin:
            own = load_row(rows_in, 1, places[0], r, channels, width, margin)
        elif r < margin + count:
            own = tile[r - margin]
        else:
            own = load_row(rows_in, 0, places[0], r - margin - count, channels, width, margin)
        if width == 64:
            own = jnp.where(lane < width, own, sides[r])
        yield r, own, sides[r]


def store_shifts(taps, r, at, step, own, sides, width, spacing):
    channels = own.shape[0]
    lane = lane_of(own.shape)
    if width == 64:
        from_left, from_right = own, own
    else:
        from_left = jnp.where(lane >= LANES - spacing, sides, own)
        from_right = jnp.where(lane < spacing, sides, own)
    taps[r, at : at + channels] = turn(from_left, spacing)
    taps[r, step + at : step + at + channels] = own
    taps[r, 2 * step + at : 2 * step + at + channels] = turn(from_right, -spacing)


def fill_taps(taps, tile, received, places, width, sc, spacing):
    channels = tile.shape[1]
    for r, own, sides in padded_rows(tile, received, places, width, DMAX, sc):
        store_shifts(taps, r, 0, channels, own, sides, width, spacing)


def tap_pair(taps, i, spacing):
    sections = []
    for row in (i, i + 1):
        sections.append(
            jnp.concatenate([taps[row + DMAX + (a - 1) * spacing] for a in range(3)], axis=0)
        )
    return jnp.concatenate(sections, axis=1)


def column_of(offset):
    return jnp.concatenate([offset[...], offset[...]], axis=1)


def normal_cdf(values):
    return 0.5 + 0.5 * lax.erf(values * (2.0**-0.5))


def gelu(values):
    return values * normal_cdf(values)


def gelu_slope(values):
    density = jnp.exp(-0.5 * values * values) * (1.0 / math.sqrt(2.0 * math.pi))
    return normal_cdf(values) + values * density


def pool_matrix(weight):
    row = lax.broadcasted_iota(jnp.int32, (2 * LANES, LANES), 0)
    col = lax.broadcasted_iota(jnp.int32, (2 * LANES, LANES), 1)
    return jnp.where(jnp.bitwise_and(row, LANES - 1) // 2 == col, weight, 0.0).astype(BF16)


def spread_matrix():
    row = lax.broadcasted_iota(jnp.int32, (LANES, LANES), 0)
    col = lax.broadcasted_iota(jnp.int32, (LANES, LANES), 1)
    return jnp.where(col // 2 == row, 1.0, 0.0).astype(BF16)


def side_spread_matrix():
    row = lax.broadcasted_iota(jnp.int32, (LANES, LANES), 0)
    col = lax.broadcasted_iota(jnp.int32, (LANES, LANES), 1)
    source = jnp.where(col >= 124, 126 + (col - 124) // 2, jnp.where(col < 4, 64 + col // 2, -1))
    return jnp.where(source == row, 1.0, 0.0).astype(BF16)


def fill_delta(delta, rows):
    count = delta.shape[0] - 16
    nothing = jnp.zeros((8,) + delta.shape[1:], BF16)
    delta[0:8] = nothing
    delta[8 + count :] = nothing
    for r in range(count):
        delta[8 + r] = rows(r)


def tap_products(delta, kernel, spacing, r):
    sections = []
    for row in (r, r + 1):
        sections.append(
            jnp.concatenate([delta[8 + row - DMAX - (a - 1) * spacing] for a in range(3)], axis=0)
        )
    return matmul(kernel[...], jnp.concatenate(sections, axis=1))


def move_taps(left, middle, right, spacing, width):
    lane = lane_of(middle.shape)
    to_left, to_right = turn(left, -spacing), turn(right, spacing)
    if width == 64:
        own = middle + to_left + to_right
        return own, own
    keep_right = lane >= spacing
    keep_left = lane < LANES - spacing
    own = middle + jnp.where(keep_right, to_right, 0.0) + jnp.where(keep_left, to_left, 0.0)
    sides = jnp.where(keep_right, 0.0, to_right) + jnp.where(keep_left, 0.0, to_left)
    return own, sides


def spread_taps(delta, kernel, spacing, width):
    count = delta.shape[0] - 16
    channels = kernel.shape[0] // 3
    for r in range(0, count + 2 * DMAX, 2):
        both = tap_products(delta, kernel, spacing, r)
        for k in range(2):
            part = both[:, k * LANES : (k + 1) * LANES]
            pieces = [part[e * channels : (e + 1) * channels] for e in range(3)]
            yield (r + k,) + move_taps(*pieces, spacing, width)


def rim_messages(own, sides, sends, places, width, margin, sc):
    rows_out = sends[0]
    total, channels = own.shape[0], own.shape[1]
    count = total - 2 * margin
    lane = lane_of((channels, LANES))
    near = []
    for first_lane in (-margin, width):
        packed = pack_columns(lambda r: sides[margin + r].astype(BF16), count, first_lane, None)
        near.append(squeeze(packed, PITCH * count))
    put_sides(sends[1:3], None, places[1], near[0], near[1], sc)
    corners = []
    for side, code, start in ((0, sc[4], 0), (1, sc[5], margin + count)):
        mirror = flipper(code, width)
        flat = own[start : start + margin].reshape(margin * channels, LANES).astype(BF16)
        turned = matmul(flat, mirror).reshape(margin, channels, LANES)
        store_rows(turned, rows_out, side, places[0], width, margin)
        if width != 64:
            flat = sides[start : start + margin].reshape(margin * channels, LANES).astype(BF16)
            turned = matmul(flat, mirror).reshape(margin, channels, LANES)
        base = short_base(code, count, margin)
        left = jnp.zeros((channels, LANES), F32)
        right = jnp.zeros((channels, LANES), F32)
        for k in range(margin):
            here = lane // PITCH == base + k
            left = jnp.where(here, turn(turned[k], PITCH * (base + k) + margin), left)
            right = jnp.where(here, turn(turned[k], PITCH * (base + k) - width), right)
        corners.append((squeeze(left, 32), squeeze(right, 32)))
    if sends[3].shape[0] == 1:
        both = [corners[0][i] + corners[1][i] for i in range(2)]
        put_sides(sends[3:5], 0, places[2], both[0], both[1], sc)
    else:
        for index in range(2):
            left, right = corners[1 - index]
            put_sides(sends[3:5], index, places[2], left, right, sc)


def fold(total, inner, received, places, width, margin, sc):
    rows_in = received[0]
    count, channels = inner.shape[0], inner.shape[1]
    lane = lane_of((channels, LANES))
    used = PITCH * count
    found = [
        side.astype(F32)
        for side in get_sides(received[1:3], None, places[1], channels, used, sc)
    ]
    for index in range(received[3].shape[0]):
        for i, short in enumerate(get_sides(received[3:5], index, places[2], channels, 32, sc)):
            short = short.astype(F32)
            if count <= 8:
                found[i] = found[i] + jnp.where(lane < 32, short, 0.0)
            else:
                late = turn(short, used - 32)
                late = jnp.where((lane >= used - 16) & (lane < used), late, 0.0)
                found[i] = found[i] + jnp.where(lane < 16, short, late)
    for r in range(count):
        row = inner[r]
        for packed, code in ((found[0], sc[2]), (found[1], sc[3])):
            first = jnp.where(odd(code) == 1, width - margin, 0)
            place = jnp.where(code >= 2, count - 1 - r, r)
            moved = turn(packed, first - PITCH * place)
            row = row + jnp.where((lane >= first) & (lane < first + margin), moved, 0.0)
        total[r] = row
    for side, code in ((0, sc[1]), (1, sc[0])):
        base = odd(code) * (count - margin)
        for k in range(margin):
            total[base + k] = total[base + k] + load_row(
                rows_in, side, places[0], k, channels, width, margin
            ).astype(F32)


START = (0, 0, 0)
AFTER_POOLED = (2, 1, 1)
AFTER_SECOND = (4, 2, 2)


def weights_kernel(jobs, swapped, *refs):
    layers = sorted({layer for _, layer in jobs})
    kernels = dict(zip(layers, refs))
    shifts = [layer for form, layer in jobs if form == 2]
    offsets = dict(zip(shifts, refs[len(layers) :]))
    outs = dict(zip(jobs, refs[len(layers) + len(shifts) :]))
    for layer in layers:
        kernel = kernels[layer]
        count, channels = kernel.shape[1:]
        if swapped[layer]:
            count, channels = channels, count
        for tap in range(9):
            a, e = tap // 3, tap % 3
            for form in range(2):
                if (form, layer) not in outs:
                    continue
                part = kernel[tap]
                if (form == 1) != swapped[layer]:
                    part = jnp.transpose(part.astype(F32)).astype(BF16)
                if form == 0:
                    outs[0, layer][:, tap * channels : (tap + 1) * channels] = part
                else:
                    rows = slice(e * channels, (e + 1) * channels)
                    outs[1, layer][rows, a * count : (a + 1) * count] = part
        if (2, layer) in outs:
            row = lax.broadcasted_iota(jnp.int32, (count, count), 0)
            col = lax.broadcasted_iota(jnp.int32, (count, count), 1)
            column = jnp.where(row == col, offsets[layer][...], 0.0)
            column = jnp.sum(column, axis=1, keepdims=True)
            outs[2, layer][...] = jnp.broadcast_to(column, outs[2, layer].shape)


def fields_kernel(sc, fields, tile, *sends):
    tile[...] = jnp.swapaxes(fields[...], 0, 1)
    edge_messages(lambda r: tile[r], tile, sends, START, LANES, DMAX, sc)
    last, shape = sends[0].shape[1] - 1, sends[0].shape[2:]
    for side in range(2):
        code = sc[side].astype(F32)
        sends[0][side, last] = jnp.broadcast_to(code, shape).astype(BF16)


def first_kernel(own_sc, tile, *refs):
    received, (kernel, offset) = refs[:5], refs[5:7]
    act_out, pre_out, pooled_out, sc, taps = refs[7:12]
    sends = refs[12:]
    last = received[0].shape[1] - 1
    for i in range(13):
        sc[i] = own_sc[i]
    for i in range(2):
        sc[4 + i] = jnp.max(received[0][1 - i, last].astype(F32)).astype(jnp.int32)
    spacing = own_sc[6]
    fill_taps(taps, tile, received, START, LANES, sc, spacing)
    pool = pool_matrix(0.25)
    shift = column_of(offset)
    for i in range(0, tile.shape[0], 2):
        pre = matmul(kernel[...], tap_pair(taps, i, spacing)) + shift
        act = gelu(pre).astype(BF16)
        for k in range(2):
            act_out[i + k] = act[:, k * LANES : (k + 1) * LANES]
            pre_out[i + k] = pre[:, k * LANES : (k + 1) * LANES]
        pooled_out[i // 2] = matmul(act, pool).astype(BF16)
    edge_messages(
        lambda r: pooled_out[r], pooled_out, sends, START, 64, DMAX, sc
    )
    edge_messages(
        lambda r: act_out[r], act_out, sends, AFTER_POOLED, LANES, DMAX, sc
    )


def second_kernel(sc, tile, *refs):
    received, (kernel, offset), extras = refs[:5], refs[5:7], refs[7:12]
    act_out, pre_out, taps = refs[12:15]
    sends = refs[15:]
    spacing = sc[7]
    fill_taps(taps, tile, received, START, 64, sc, spacing)
    shift = column_of(offset)
    for i in range(0, tile.shape[0], 2):
        pre = matmul(kernel[...], tap_pair(taps, i, spacing)) + shift
        act = gelu(pre).astype(BF16)
        for k in range(2):
            act_out[i + k] = act[:, k * LANES : (k + 1) * LANES]
            pre_out[i + k] = pre[:, k * LANES : (k + 1) * LANES]
    edge_messages(lambda r: act_out[r], act_out, sends, START, 64, DMAX, sc)
    pass_on(extras, sends, AFTER_SECOND)


def slopes_kernel(*refs):
    half = len(refs) // 2
    for values, out in zip(refs[:half], refs[half:]):
        for r in range(values.shape[0]):
            out[r] = gelu_slope(values[r])


def masked(values, width):
    return jnp.where(lane_of(values.shape) < width, values, 0.0).astype(BF16)


def back_part(sc, delta, kernel, spacing, width, inner_out, sends, own_all, sides_all):
    count = delta.shape[0] - 16
    for r, own, sides in spread_taps(delta, kernel, spacing, width):
        own_all[r] = own
        if width != 64:
            sides_all[r] = sides
    for r in range(count):
        inner_out[r] = own_all[DMAX + r]
    rim_messages(own_all, sides_all, sends, START, width, DMAX, sc)


def third_kernel(sc, tile, *refs):
    received, (kernel, offset, coarse, back) = refs[:5], refs[5:9]
    act_out, delta_out, inner_out = refs[9:12]
    sends, (taps, delta, own_all, coarse_sum) = refs[12:17], refs[17:]
    fold(coarse_sum, coarse, received, AFTER_SECOND, 64, 2, sc)
    spacing = sc[8]
    fill_taps(taps, tile, received, START, 64, sc, spacing)
    shift = column_of(offset)
    for i in range(0, tile.shape[0], 2):
        pre = matmul(kernel[...], tap_pair(taps, i, spacing)) + shift
        act, slope = gelu(pre), gelu_slope(pre)
        for k in range(2):
            act_out[i + k] = act[:, k * LANES : (k + 1) * LANES].astype(BF16)
            delta_out[i + k] = masked(
                coarse_sum[i + k] * slope[:, k * LANES : (k + 1) * LANES], 64
            )
    fill_delta(delta, lambda r: delta_out[r])
    back_part(sc, delta, back, spacing, 64, inner_out, sends, own_all, own_all)
    edge_messages(lambda r: act_out[r], act_out, sends, AFTER_SECOND, 64, 2, sc)


def middle_kernel(sc, inner, *refs):
    received, (slope, back), extras = refs[:5], refs[5:7], refs[7:12]
    delta_out, inner_out = refs[12:14]
    sends, (total, delta, own_all) = refs[14:19], refs[19:]
    fold(total, inner, received, START, 64, DMAX, sc)
    for r in range(inner.shape[0]):
        delta_out[r] = masked(total[r] * slope[r], 64)
    fill_delta(delta, lambda r: delta_out[r])
    back_part(sc, delta, back, sc[7], 64, inner_out, sends, own_all, own_all)
    pass_on(extras, sends, AFTER_POOLED)


def lower_kernel(sc, inner, *refs):
    received, (slope, skip_inner, back) = refs[:5], refs[5:8]
    delta_out, inner_out = refs[8:10]
    sends, (total, skip, delta, own_all, sides_all) = refs[10:15], refs[15:]
    fold(total, inner, received, START, 64, DMAX, sc)
    fold(skip, skip_inner, received, AFTER_POOLED, LANES, DMAX, sc)
    spread = spread_matrix()
    for r in range(inner.shape[0]):
        lane = lane_of(total[r].shape)
        high, low = halves(jnp.where(lane < 64, total[r], 0.0))
        wide = 0.25 * (matmul(high, spread) + matmul(low, spread))
        for k in range(2):
            row = 2 * r + k
            delta_out[row] = ((skip[row] + wide) * slope[row]).astype(BF16)
    fill_delta(delta, lambda r: delta_out[r])
    back_part(sc, delta, back, sc[6], LANES, inner_out, sends, own_all, sides_all)


def last_kernel(sc, inner, *refs):
    received, out, total = refs[:5], refs[5], refs[6]
    fold(total, inner, received, START, LANES, DMAX, sc)
    out[...] = jnp.swapaxes(total[...], 0, 1)


def moved_pool_matrix(spacing):
    row = lax.broadcasted_iota(jnp.int32, (2 * LANES, LANES), 0)
    col = lax.broadcasted_iota(jnp.int32, (2 * LANES, LANES), 1)
    parts = []
    for e in range(3):
        target = jnp.right_shift(jnp.bitwise_and(row, LANES - 1) + (e - 1) * spacing, 1)
        hit = jnp.bitwise_and(target, LANES - 1) == col
        parts.append(jnp.where(hit, 1.0, 0.0).astype(BF16))
    return jnp.concatenate(parts, axis=0)


def upstream_kernel(sc, cotangent, closing, *refs):
    upstream, coarse_out, skip_out = refs[:3]
    coarse_sends, skip_sends = refs[3:8], refs[8:13]
    delta, own_all, sides_all, coarse_all, back, high_all, low_all = refs[13:]
    outs, channels = closing.shape[1:]
    for tap in range(9):
        a, e = tap // 3, tap % 3
        across = jnp.transpose(closing[tap].astype(F32)).astype(BF16)
        back[e * channels : (e + 1) * channels, a * outs : (a + 1) * outs] = across
    upstream[...] = jnp.swapaxes(cotangent[...], 0, 1)
    fill_delta(delta, lambda r: upstream[r])
    spacing = sc[9]
    pool = moved_pool_matrix(spacing)
    skips = own_all.shape[1]
    coarse = channels - skips
    for r in range(0, own_all.shape[0], 2):
        both = tap_products(delta, back, spacing, r)
        parts = [both[e * channels : (e + 1) * channels] for e in range(3)]
        high, low = halves(jnp.concatenate([part[:coarse] for part in parts], axis=1))
        at = r // 2 * coarse
        high_all[at : at + coarse] = high
        low_all[at : at + coarse] = low
        for k in range(2):
            lanes = slice(k * LANES, (k + 1) * LANES)
            own, sides = move_taps(*[part[coarse:, lanes] for part in parts], spacing, LANES)
            own_all[r + k] = own
            sides_all[r + k] = sides
    pooled = matmul(high_all[...], pool) + matmul(low_all[...], pool)
    coarse_all[...] = pooled.reshape(coarse_all.shape)
    for r in range(coarse_out.shape[0]):
        coarse_out[r] = coarse_all[2 + r]
    for r in range(skip_out.shape[0]):
        skip_out[r] = own_all[4 + r]
    rim_messages(coarse_all, coarse_all, coarse_sends, START, 64, 2, sc)
    rim_messages(own_all, sides_all, skip_sends, START, LANES, 4, sc)


def put_terms(out, at, sums, sides):
    outs, columns = sums.shape
    whole = columns // LANES
    for k in range(whole):
        out[at + k * outs : at + (k + 1) * outs] = sums[:, k * LANES : (k + 1) * LANES].astype(BF16)
    if columns % LANES:
        wide = jnp.concatenate(
            [jnp.broadcast_to(side, (outs, 64 // len(sides))) for side in sides], axis=1
        )
        tail = jnp.concatenate([sums[:, whole * LANES :], wide], axis=1)
        out[at + whole * outs : at + (whole + 1) * outs] = tail.astype(BF16)


def row_sum(rows):
    total = None
    for r in range(rows.shape[0]):
        row = rows[r].astype(F32)
        total = row if total is None else total + row
    return jnp.sum(total, axis=1, keepdims=True)


def layer_terms(taps, delta, spacing, use=None):
    sums = None
    for i in range(0, delta.shape[0], 2):
        section = tap_pair(taps, i, spacing)
        if use is not None:
            use(i, section)
        part = matmul_t(jnp.concatenate([delta[i], delta[i + 1]], axis=1), section)
        sums = part if sums is None else sums + part
    return sums


def third_terms_kernel(sc, second, delta, *refs):
    third_in, (out, taps) = refs[:5], refs[5:]
    fill_taps(taps, second, third_in, START, 64, sc, sc[8])
    put_terms(out, 0, layer_terms(taps, delta, sc[8]), None)


def joined_kernel(
    sc, coarse, fine, taps_second, delta_third, delta_second, upstream, kernel, offset, *refs
):
    second_in, back_in = refs[:5], refs[5:10]
    state_out, out, taps, state_all = refs[10:]
    sums = layer_terms(taps_second, delta_second, sc[7])
    put_terms(out, 0, sums, [row_sum(delta_second), row_sum(delta_third)])
    after = -(-sums.shape[1] // LANES) * sums.shape[0]
    spacing = sc[9]
    spread = jnp.concatenate([spread_matrix(), side_spread_matrix()], axis=1)
    for r, own, _ in padded_rows(coarse, back_in, AFTER_SECOND, 64, 2, sc):
        wide = matmul(own, spread).astype(BF16)
        for k in range(2):
            store_shifts(
                taps, 2 * r + k, 0, 192, wide[:, :LANES], wide[:, LANES:], LANES, spacing
            )
    for r, own, sides in padded_rows(fine, second_in, AFTER_POOLED, LANES, 4, sc):
        store_shifts(taps, r, 128, 192, own, sides, LANES, spacing)
    shift = column_of(offset)

    def use(i, section):
        state = (matmul(kernel[...], section) + shift).astype(BF16)
        for k in range(2):
            state_all[i + k] = state[:, k * LANES : (k + 1) * LANES]

    put_terms(out, after, layer_terms(taps, upstream, spacing, use), [row_sum(upstream)])
    state_out[...] = jnp.swapaxes(state_all[...], 0, 1)


def first_terms_kernel(sc, taps, delta, third_terms, terms, give, keep, whole):
    rows = 0
    for part in (third_terms, terms):
        whole[rows : rows + part.shape[0]] = part[...]
        rows += part.shape[0]
    sums = layer_terms(taps, delta, sc[6])
    put_terms(whole, rows, sums, [row_sum(delta)])
    rows += -(-sums.shape[1] // LANES) * sums.shape[0]
    whole[rows:] = jnp.zeros((whole.shape[0] - rows, LANES), BF16)
    half = keep.shape[0]
    keep[...] = whole[pl.ds(pl.multiple_of(sc[10] * half, 16), half)]
    give[...] = whole[pl.ds(pl.multiple_of((1 - sc[10]) * half, 16), half)]


def core_sum_kernel(sc, keep, given, own, *gives):
    size = own.shape[0]
    for i, out in enumerate((own,) + gives):
        member = sc[11] if i < 2 else 1 - sc[11]
        chip = sc[12] if i % 2 == 0 else 1 - sc[12]
        rows = pl.ds(pl.multiple_of((2 * member + chip) * size, 16), size)
        out[...] = (keep[rows].astype(F32) + given[rows].astype(F32)).astype(out.dtype)


def adding_kernel(*refs):
    total = refs[0][...].astype(F32)
    for ref in refs[1:-1]:
        total = total + ref[...].astype(F32)
    refs[-1][...] = total.astype(BF16)


def unpack_kernel(scale, layouts, biases, sc, *refs):
    eighths, outs, summed = refs[:8], refs[8:-1], refs[-1]
    size = eighths[0].shape[0]
    for i, eighth in enumerate(eighths):
        bits = [sc[10 + k] if (i >> (2 - k)) % 2 == 0 else 1 - sc[10 + k] for k in range(3)]
        at = pl.multiple_of((4 * bits[0] + 2 * bits[1] + bits[2]) * size, 16)
        summed[pl.ds(at, size)] = eighth[...]
    for (start, outs_count, channels, swapped), out in zip(layouts, outs):
        def slab_at(slab):
            first = start + slab * outs_count
            return summed[first : first + outs_count].astype(F32) * scale

        if swapped:
            for slab in range(5):
                across = jnp.transpose(slab_at(slab))
                for tap in range(2 * slab, min(2 * slab + 2, 9)):
                    at = (tap - 2 * slab) * channels
                    out[tap] = across[at : at + channels]
            continue
        for tap in range(9):
            first, last = tap * channels, (tap + 1) * channels
            found = []
            while first < last:
                slab = first // LANES
                end = min(last, (slab + 1) * LANES)
                found.append(slab_at(slab)[:, first - slab * LANES : end - slab * LANES])
                first = end
            out[tap] = found[0] if len(found) == 1 else jnp.concatenate(found, axis=1)
    for (start, count, lane), out in zip(biases, outs[len(layouts) :]):
        block = summed[start : start + count].astype(F32)
        column = jnp.sum(
            jnp.where(lane_of(block.shape) == lane, block, 0.0), axis=1, keepdims=True
        )
        row = lax.broadcasted_iota(jnp.int32, (count, count), 0)
        col = lax.broadcasted_iota(jnp.int32, (count, count), 1)
        out[...] = jnp.sum(jnp.where(row == col, column, 0.0), axis=0, keepdims=True) * scale


def call(body, inputs, outputs, scratch=(), flops=0, scalars=1, name=None):
    specs = [pl.BlockSpec(memory_space=pltpu.VMEM)] * len(inputs)
    for i in range(scalars):
        specs[i] = pl.BlockSpec(memory_space=pltpu.SMEM)
    moved = sum(math.prod(shape) * jnp.dtype(kind).itemsize for shape, kind in outputs)
    moved += sum(array.size * array.dtype.itemsize for array in inputs)
    spaces = [pltpu.SMEM if kind == jnp.int32 else pltpu.VMEM for _, kind in outputs]
    return pl.pallas_call(
        body,
        out_shape=[jax.ShapeDtypeStruct(shape, kind) for shape, kind in outputs],
        in_specs=specs,
        out_specs=[pl.BlockSpec(memory_space=space) for space in spaces],
        scratch_shapes=[pltpu.VMEM(shape, kind) for shape, kind in scratch],
        compiler_params=pltpu.CompilerParams(vmem_limit_bytes=24 * 1024 * 1024),
        cost_estimate=pl.CostEstimate(flops=flops, bytes_accessed=moved, transcendentals=0),
        name=name,
    )(*inputs)


def shifted(array, for_even, for_odd):
    devices = lax.axis_size("tile")
    pairs = [(i, (i + (for_odd if i % 2 else for_even)) % devices) for i in range(devices)]
    return lax.ppermute(array, "tile", pairs)


def wrapped():
    return lax.axis_size("tile") == 2 * TILE_ROW


def other_tile(array, bit):
    pairs = [(i, i ^ (1 << bit)) for i in range(lax.axis_size("tile"))]
    return lax.ppermute(array, "tile", pairs)


def other_member(array):
    return lax.ppermute(array, "ens", [(0, 1), (1, 0)])


def other_both(array, bit):
    tiles = lax.axis_size("tile")
    pairs = [(i, (i ^ (1 << bit)) + tiles if i < tiles else (i ^ (1 << bit)) - tiles)
             for i in range(2 * tiles)]
    return lax.ppermute(array, ("ens", "tile"), pairs)


def exchange_rows(rows):
    if wrapped():
        return shifted(rows, TILE_ROW, TILE_ROW)
    return jnp.stack(
        [shifted(rows[0], -TILE_ROW, -TILE_ROW), shifted(rows[1], TILE_ROW, TILE_ROW)]
    )


def exchange(rows, near_a, near_b, far_a, far_b):
    row = TILE_ROW
    rows_in = exchange_rows(rows)
    if wrapped():
        a_in = shifted(far_a, row + 1, row - 1)
        b_in = shifted(far_b, row - 1, row + 1)
    else:
        a_in = jnp.stack(
            [shifted(far_a[0], row + 1, row - 1), shifted(far_a[1], 1 - row, -1 - row)]
        )
        b_in = jnp.stack(
            [shifted(far_b[0], row - 1, row + 1), shifted(far_b[1], -1 - row, 1 - row)]
        )
    return [rows_in, shifted(near_a, 1, -1), shifted(near_b, -1, 1), a_in, b_in]


def shards(
    fields,
    cotangent,
    kernel_first,
    kernel_second,
    kernel_third,
    closing_filter_weights,
    offset_first,
    offset_second,
    offset_third,
    closing_shift_values,
    codes,
    filter_stride_spread,
):
    members, _, low, height, width = fields.shape
    high = kernel_third.shape[1]
    half = height // 2
    fars = 1 if wrapped() else 2
    tile_index = lax.axis_index("tile")
    place = [tile_index & 1, lax.axis_index("ens") & 1, (tile_index >> 1) & 1]
    own_sc = jnp.concatenate(
        [codes[0], jnp.zeros((2,), jnp.int32), filter_stride_spread]
        + [bit.astype(jnp.int32)[None] for bit in place]
    )

    def sends(rows, near, far):
        return (
            [((2, rows, 64, LANES), BF16)]
            + [((near, 16, LANES), BF16)] * 2
            + [((fars, far, 16, LANES), BF16)] * 2
        )

    fine_tile = ((height, low, LANES), BF16)
    fine_grad = ((height, low, LANES), F32)
    tile, *sent = call(
        fields_kernel,
        [own_sc, fields[0, 0]],
        [fine_tile, ((2, DMAX * low // 16 + 1, 16, LANES), BF16)] + sends(5, 2, 1)[1:],
        name="fields_edges",
    )
    first_in = exchange(*sent)

    weights = [kernel_first, kernel_second, kernel_third, closing_filter_weights]
    offsets = [offset_first, offset_second, offset_third, closing_shift_values]
    swapped = [k.shape[1] % LANES == 0 and k.shape[2] % LANES != 0 for k in weights]
    def prepare(jobs, kernels, name):
        layers = sorted({layer for _, layer in jobs})
        inputs = [jnp.swapaxes(kernels[i], 1, 2) if swapped[i] else kernels[i] for i in layers]
        outputs = []
        for form, layer in jobs:
            _, count, channels = kernels[layer].shape
            shapes = [(count, 9 * channels), (3 * channels, 3 * count), (count, LANES)]
            outputs.append((shapes[form], F32 if form == 2 else BF16))
        made = call(
            functools.partial(weights_kernel, jobs, swapped),
            inputs + [offsets[layer][None] for form, layer in jobs if form == 2],
            outputs,
            scalars=0,
            name=name,
        )
        return dict(zip(jobs, made))

    forms = prepare([(0, 0), (0, 1), (2, 0), (2, 1)], weights, "early_weights")

    first_taps = ((height + 8, 3 * low, LANES), BF16)
    act_first, pre_first, pooled, sc, taps_first, *sent = call(
        first_kernel,
        [own_sc, tile, *first_in, forms[0, 0], forms[2, 0]],
        [fine_tile, fine_grad, ((half, low, LANES), BF16), ((13,), jnp.int32), first_taps]
        + sends(6, 3, 2),
        flops=2 * 9 * low * low * height * width,
        name="first_layer",
    )
    second_in = exchange(*sent)

    upstream, coarse_inner, skip_inner, *rims = call(
        upstream_kernel,
        [sc, cotangent[0, 0], closing_filter_weights],
        [fine_tile, ((half, high, LANES), F32), fine_grad] + sends(2, 2, 2) + sends(4, 2, 1),
        [
            ((height + 16, low, LANES), BF16),
            ((height + 8, low, LANES), F32),
            ((height + 8, low, LANES), F32),
            ((half + 4, high, LANES), F32),
            ((3 * (low + high), 3 * low), BF16),
            (((half + 4) * high, 6 * LANES), BF16),
            (((half + 4) * high, 6 * LANES), BF16),
        ],
        flops=2 * 9 * low * (low + high) * height * width,
        name="cotangent_back",
    )
    coarse_rims, skip_rims = rims[:5], rims[5:]

    second_taps = ((half + 8, 3 * low, LANES), BF16)
    act_second, pre_second, taps_second, *sent = call(
        second_kernel,
        [sc, pooled, *second_in, forms[0, 1], forms[2, 1], *coarse_rims],
        [((half, high, LANES), BF16), ((half, high, LANES), F32), second_taps]
        + sends(6, 4, 4),
        flops=2 * 9 * low * high * half * LANES,
        name="second_layer",
    )
    third_in = exchange(*sent)
    late_third, pre_second = lax.optimization_barrier((kernel_third, pre_second))
    forms.update(
        prepare(
            [(0, 2), (0, 3), (1, 0), (1, 1), (1, 2), (2, 2), (2, 3)],
            weights[:2] + [late_third] + weights[3:],
            "late_weights",
        )
    )
    slope_first, slope_second = call(
        slopes_kernel,
        [pre_first, pre_second],
        [fine_grad, ((half, high, LANES), F32)],
        scalars=0,
        name="slopes",
    )
    coarse_inner, slope_first = lax.optimization_barrier((coarse_inner, slope_first))

    third_taps = ((half + 8, 3 * high, LANES), BF16)
    act_third, delta_third, inner, *sent = call(
        third_kernel,
        [sc, act_second, *third_in, forms[0, 2], forms[2, 2], coarse_inner, forms[1, 2]],
        [((half, high, LANES), BF16)] * 2 + [((half, high, LANES), F32)] + sends(6, 4, 4),
        [
            third_taps,
            ((half + 16, high, LANES), BF16),
            ((half + 8, high, LANES), F32),
            ((half, high, LANES), F32),
        ],
        flops=2 * 2 * 9 * high * high * half * LANES,
        name="third_layer_and_back",
    )
    back_in = exchange(*sent)
    (third_terms,) = call(
        third_terms_kernel,
        [sc, act_second, delta_third, *third_in],
        [((9 * high, LANES), BF16)],
        [third_taps],
        flops=2 * 9 * high * high * half * LANES,
        name="third_terms",
    )
    inner, third_terms = lax.optimization_barrier((inner, third_terms))

    delta_second, inner, *sent = call(
        middle_kernel,
        [sc, inner, *back_in, slope_second, forms[1, 1], *skip_rims],
        [((half, high, LANES), BF16), ((half, low, LANES), F32)] + sends(6, 3, 2),
        [
            ((half, high, LANES), F32),
            ((half + 16, high, LANES), BF16),
            ((half + 8, low, LANES), F32),
        ],
        flops=2 * 9 * low * high * half * LANES,
        name="second_back",
    )
    lower_in = exchange(*sent)

    narrow = -(-9 * low // LANES)
    wide = -(-9 * (low + high) // LANES)
    upper_rows = narrow * high + wide * low
    state, upper_terms = call(
        joined_kernel,
        [
            sc, act_third, act_first, taps_second, delta_third, delta_second, upstream, forms[0, 3],
            forms[2, 3], *second_in, *back_in,
        ],
        [((low, height, LANES), BF16), ((upper_rows, LANES), BF16)],
        [
            ((height + 8, 3 * (low + high), LANES), BF16),
            fine_tile,
        ],
        flops=2 * 2 * 9 * low * (low + high) * height * width,
        name="joined_layer_and_terms",
    )
    lower_in[0], upper_terms = lax.optimization_barrier((lower_in[0], upper_terms))

    delta_first, inner, *sent = call(
        lower_kernel,
        [sc, inner, *lower_in, slope_first, skip_inner, forms[1, 0]],
        [fine_tile, fine_grad] + sends(4, 2, 1),
        [
            ((half, low, LANES), F32),
            fine_grad,
            ((height + 16, low, LANES), BF16),
            ((height + 8, low, LANES), F32),
            ((height + 8, low, LANES), F32),
        ],
        flops=2 * 9 * low * low * height * width,
        name="first_back",
    )

    tiles = lax.axis_size("tile")
    rows = 9 * high + upper_rows + narrow * low
    size = -(-rows // (8 * 16)) * 16

    def part(count):
        return ((count * size, LANES), BF16)

    give, keep = call(
        first_terms_kernel,
        [sc, taps_first, delta_first, third_terms, upper_terms],
        [part(4)] * 2,
        [part(8)],
        flops=2 * 9 * low * low * height * width,
        name="first_terms",
    )
    given = other_tile(give, 0)
    own, *gives = call(
        core_sum_kernel,
        [sc, keep, given],
        [((size, LANES), F32)] + [part(1)] * 3,
        name="core_sum",
    )
    given = [other_tile(gives[0], 1), other_member(gives[1]), other_both(gives[2], 1)]
    last_in = exchange(*sent)
    own, *last_in[:3] = lax.optimization_barrier((own, *last_in[:3]))
    (total,) = call(adding_kernel, [own, *given], [part(1)], scalars=0, name="chip_sum")
    for bit in range(2, tiles.bit_length() - 1):
        given = other_tile(total, bit)
        (total,) = call(adding_kernel, [total, given], [part(1)], scalars=0, name=f"sum_{bit}")
    (derivative,) = call(
        last_kernel,
        [sc, inner, *last_in],
        [((low, height, LANES), F32)],
        [fine_grad],
        name="last_fold",
    )

    total, derivative = lax.optimization_barrier((total, derivative))
    eighths = [total, other_tile(total, 1), other_member(total), other_both(total, 1)]
    eighths = eighths + [other_tile(eighth, 0) for eighth in eighths]

    all_tiles = members * lax.axis_size("ens") * lax.axis_size("tile")
    scale = 1.0 / math.sqrt(all_tiles * height * width)
    upper_rows += 9 * high
    starts = [upper_rows, 9 * high, 0, upper_rows - wide * low]
    layouts = [
        (start, k.shape[1], k.shape[2], swap) for start, k, swap in zip(starts, weights, swapped)
    ]
    tail = 9 * high + (narrow - 1) * high
    biases = [(rows - low, low, 64), (tail, high, 64), (tail, high, 96), (upper_rows - low, low, 64)]
    grads = call(
        functools.partial(unpack_kernel, scale, layouts, biases),
        [sc, *eighths],
        [
            ((9, channels, outs) if swap else (9, outs, channels), F32)
            for _, outs, channels, swap in layouts
        ]
        + [((1, count), F32) for _, count, _ in biases],
        [part(8)],
        name="unpack_sums",
    )
    return (
        state[None, None],
        derivative[None, None],
        *[jnp.swapaxes(g, 1, 2) if swap else g for g, swap in zip(grads[:4], swapped)],
        *[grad[0] for grad in grads[4:]],
    )


def solution(mesh):
    tiles = P("ens", "tile", None, None, None)
    in_specs = (tiles, tiles) + (P(),) * 8 + (P("tile", None), P())
    out_specs = (tiles, tiles) + (P(),) * 8
    return jax.shard_map(shards, mesh=mesh, in_specs=in_specs, out_specs=out_specs, check_vma=False)
```
